32 devices in a mesh: grid: 4 (over y, core), tile: 8 (over z, x).
Axes of the slice: x: 2, y: 2, z: 4, core: 2. Of those that a mesh axis runs over, the one named last changes fastest.
Arguments:
- rhs_local: bfloat16 [192, 49152], P(None, ('grid', 'tile')), may hold values from -6 to 6
- diag_inv: bfloat16 [96, 512, 512], P(('grid', 'tile')), may hold values from -1 to 2, as said below
- codes: bfloat16 [20480, 1536], P(('grid', 'tile')), may hold values from -127 to 127, as said below
- row_scales: float32 [20480], P(('grid', 'tile')), may hold values from 0 to 1, as said below
- sep_index: int32 [20480], P(('grid', 'tile')), may hold values from 0 to 2559, as said below
- live_rows: int32 [32], P(('grid', 'tile')), may hold values from 160 to 640, as said below
- rhs_sep: bfloat16 [192, 2560], P(None, 'tile'), may hold values from -6 to 6
- root_inv: bfloat16 [2560, 2560], P('tile'), may hold values from -1 to 2, as said below
Outputs:
- solution_local: bfloat16 [192, 49152], P(None, ('grid', 'tile'))
- solution_sep: float32 [192, 2560], P(None, 'tile')
The draws below stay inside these ranges and needn't reach their ends.
Inputs may be any that keep to these rules, and one draw needn't show every extreme that they name: `diag_inv`: each block is upper triangular. `root_inv`: each block is upper triangular. `codes`: Integers. `row_scales`: Positive. `sep_index`: of each device's 640 entries, the j-th run of 80 consecutive entries lies in j * 320 to (j + 1) * 320 - 1, and the entries of one run are distinct. `live_rows`: some device has all 640 rows live.
All inputs are finite; a program needn't handle non-finite values.
Results may differ from the reference program's by a relative error of at most 0.0054.
Values may be sent and summed in bfloat16 or wider, within the bound.
A program may use at most 64 MiB of HBM per device.

```python
import math
import jax
import jax.numpy as jnp
from jax import lax

RHS = 192
BLOCK = 512
PER_DEV = 3
CROWS = 640
SEP = 2560
LOCAL = 1536
MEMBERS = 32
BLOCKS = 96
COUPLED = 20480
UNKNOWNS = 49152
N_TILE = 8


def upper_blocks(key, count, order):
    keys = jax.random.split(key, 2)
    diagonal = jax.random.uniform(keys[0], (count, order), jnp.float32, 0.7, 1.3)
    upper = jax.random.normal(keys[1], (count, order, order), jnp.float32) * (0.6 / math.sqrt(order))
    upper = jnp.clip(upper, -0.9, 0.9)
    strict = jnp.triu(jnp.ones((order, order), jnp.float32), 1)
    eye = jnp.eye(order, dtype=jnp.float32)
    return upper * strict[None] + diagonal[:, :, None] * eye[None]


def draw_diag_inv(key, part):
    return upper_blocks(key, BLOCKS, BLOCK).astype(jnp.bfloat16)


def draw_root_inv(key, part):
    return upper_blocks(key, 1, SEP)[0].astype(jnp.bfloat16)


def draw_codes(key, part):
    values = jax.random.randint(key, (COUPLED, LOCAL), -127, 128)
    return values.astype(jnp.float32).astype(jnp.bfloat16)


def draw_row_scales(key, part):
    spread = jax.random.uniform(key, (COUPLED,), jnp.float32, math.log(0.2), math.log(2.0))
    norming = 73.0 * math.sqrt(LOCAL * COUPLED / SEP)
    return (jnp.exp(spread) / norming).astype(jnp.float32)


def draw_sep_index(key, part):
    share_len = SEP // N_TILE
    per_share = CROWS // N_TILE
    keys = jax.random.split(key, MEMBERS * N_TILE)
    picks = jax.vmap(lambda member_key: jax.random.permutation(member_key, share_len)[:per_share])(keys)
    picks = picks.reshape(MEMBERS, N_TILE, per_share).astype(jnp.int32)
    starts = (jnp.arange(N_TILE, dtype=jnp.int32) * share_len)[None, :, None]
    return (picks + starts).reshape(COUPLED).astype(jnp.int32)


def draw_live_rows(key, part):
    keys = jax.random.split(key, 2)
    counts = jax.random.randint(keys[0], (MEMBERS,), max(1, CROWS // 4), CROWS + 1)
    chosen = jax.random.randint(keys[1], (), 0, MEMBERS)
    return counts.at[chosen].set(CROWS).astype(jnp.int32)


def steps_of(stream_key, extent, cuts, smallest, high):
    def one(dim, blocks):
        draws = jax.random.uniform(jax.random.fold_in(jax.random.fold_in(stream_key, 6), dim), (blocks,), jnp.float32, smallest / len(cuts), high / len(cuts))
        return jnp.repeat(jnp.exp(draws), extent[dim] // blocks).reshape((-1,) + (1,) * (len(extent) - dim - 1))

    level = one(*cuts[0])
    for cut in cuts[1:]:
        level = level * one(*cut)
    return level


def gaussian(stream_key, extent, deviation, bound, pieces=(), kind=jnp.bfloat16):
    drawn = jax.random.normal(stream_key, extent, jnp.float32) * deviation
    if len(pieces) > 0:
        drawn = steps_of(stream_key, extent, pieces, -0.22, 0.18) * drawn
    return jnp.clip(drawn, min=-bound, max=bound).astype(kind)


def setup_inputs(seed: int = 0) -> dict:
    seeds = jax.random.split(jax.random.key(seed), 9)
    return {
        "rhs_local": gaussian(seeds[0], (RHS, UNKNOWNS), 1.0, 6.0, ((1, 32),)),
        "diag_inv": draw_diag_inv(jax.random.fold_in(seeds[8], 71), 0),
        "codes": draw_codes(jax.random.fold_in(seeds[8], 71), 0),
        "row_scales": draw_row_scales(jax.random.fold_in(seeds[8], 71), 0),
        "sep_index": draw_sep_index(jax.random.fold_in(seeds[8], 71), 0),
        "live_rows": draw_live_rows(jax.random.fold_in(seeds[8], 71), 0),
        "rhs_sep": gaussian(seeds[6], (RHS, SEP), 1.0, 6.0, ((1, 8),)),
        "root_inv": draw_root_inv(jax.random.fold_in(seeds[8], 71), 0),
    }


def product(left, right):
    return jnp.dot(left.astype(jnp.float32), right.astype(jnp.float32), precision=lax.Precision.HIGHEST)


def reference(rhs_local, diag_inv, codes, row_scales, sep_index, live_rows, rhs_sep, root_inv):
    rhs_parts = rhs_local.reshape(RHS, MEMBERS, PER_DEV, BLOCK).transpose(1, 0, 2, 3)
    inv_parts = diag_inv.reshape(MEMBERS, PER_DEV, BLOCK, BLOCK)
    code_parts = codes.reshape(MEMBERS, CROWS, LOCAL)
    scale_parts = row_scales.reshape(MEMBERS, CROWS)
    index_parts = sep_index.reshape(MEMBERS, CROWS)
    positions = jnp.arange(CROWS, dtype=jnp.int32)
    factors = scale_parts * (positions[None, :] < live_rows[:, None]).astype(jnp.float32)

    def forward_step(summed, items):
        blocked, inverse, coded, row_factor, indices = items
        forward = jnp.einsum('rkb,kbc->rkc', blocked.astype(jnp.float32), inverse.astype(jnp.float32),
                             precision=lax.Precision.HIGHEST).astype(jnp.bfloat16).reshape(RHS, LOCAL)
        coupled = product(forward, coded.T) * row_factor[None, :]
        summed = summed.at[:, indices].add(coupled)
        return summed, forward

    summed, forwards = lax.scan(forward_step, jnp.zeros((RHS, SEP), jnp.float32),
                                (rhs_parts, inv_parts, code_parts, factors, index_parts))
    residue = (rhs_sep.astype(jnp.float32) - summed).astype(jnp.bfloat16)
    forward_sep = product(residue, root_inv).astype(jnp.bfloat16)
    solution_sep = product(forward_sep, root_inv.T)
    rounded_sep = solution_sep.astype(jnp.bfloat16)

    def backward_step(items):
        forward, inverse, coded, row_factor, indices = items
        picked = rounded_sep[:, indices]
        weighted = (picked.astype(jnp.float32) * row_factor[None, :]).astype(jnp.bfloat16)
        update = product(weighted, coded)
        misfit = (forward.astype(jnp.float32) - update).astype(jnp.bfloat16).reshape(RHS, PER_DEV, BLOCK)
        result = jnp.einsum('rkc,kbc->rkb', misfit.astype(jnp.float32), inverse.astype(jnp.float32),
                            precision=lax.Precision.HIGHEST).astype(jnp.bfloat16)
        return result.reshape(RHS, LOCAL)

    results = lax.map(backward_step, (forwards, inv_parts, code_parts, factors, index_parts))
    solution_local = results.transpose(1, 0, 2).reshape(RHS, UNKNOWNS)
    return solution_local, solution_sep
```

```python
import functools

import jax
import jax.numpy as jnp
from jax import lax
from jax.experimental import pallas as pl
from jax.experimental.pallas import tpu as pltpu
from jax.sharding import PartitionSpec as P

LANES = 128
ROWS = 16
MESH = pl.DeviceIdType.MESH
F32 = jnp.float32
BF16 = jnp.bfloat16
NT = (((1,), (1,)), ((), ()))


def lane_window(block, width):
    return block * width // LANES * LANES


def kernel(
    groups,
    tiles,
    factor_ref,
    index_ref,
    rhs_sep_ref,
    rhs_hbm,
    diag_hbm,
    codes_hbm,
    root_hbm,
    out_ref,
    sep_ref,
    rhs,
    diag,
    codes,
    root,
    forward,
    coupled,
    index_all,
    onehot,
    got,
    part,
    part_got,
    fsep,
    solved,
    picked,
    pick_got,
    load_sem,
    code_sem,
    self_sem,
    idx_send,
    idx_recv,
    a_send,
    a_recv,
    r_send,
    r_recv,
    f_send,
    f_recv,
    s_send,
    s_recv,
    b_send,
    b_recv,
):
    g = lax.axis_index("grid")
    t = lax.axis_index("tile")
    count = groups * tiles
    me = g * tiles + t
    per_dev, block_len = diag.shape[0], diag.shape[1]
    share = root.shape[0]
    window = part.shape[2]
    per_share = codes_hbm.shape[0] // tiles
    rhs_count = rhs.shape[0]
    rpg = rhs_count // groups
    chunk = 2
    chunks = tiles // chunk
    wide = chunk * LANES

    def lanes(position, size=LANES):
        return pl.ds(pl.multiple_of(position * LANES, LANES), size)

    def rows_of(group):
        return pl.ds(pl.multiple_of(group * rpg, ROWS), rpg)

    barrier = pltpu.get_barrier_semaphore()

    def greet(k, carry):
        peer = lax.rem(me + k, count)
        pl.semaphore_signal(
            barrier, inc=1, device_id=(peer // tiles, lax.rem(peer, tiles)), device_id_type=MESH
        )
        return carry

    lax.fori_loop(1, count, greet, 0)

    loads = [pltpu.make_async_copy(rhs_hbm, rhs, load_sem.at[0])]
    for b in range(per_dev):
        loads.append(pltpu.make_async_copy(diag_hbm.at[b], diag.at[b], load_sem.at[1 + b]))
    for load in loads:
        load.start()
    code_loads = []
    for j in range(tiles):
        code_loads.append(
            pltpu.make_async_copy(
                codes_hbm.at[pl.ds(j * per_share, per_share)],
                codes.at[pl.ds(j * LANES, per_share)],
                code_sem.at[j],
            )
        )
    for load in code_loads:
        load.start()
    root_load = pltpu.make_async_copy(root_hbm, root, load_sem.at[1 + per_dev])
    root_load.start()
    if per_share < LANES:
        for j in range(tiles):
            codes[j * LANES + per_share : (j + 1) * LANES, :] = jnp.zeros(
                (LANES - per_share, codes.shape[1]), BF16
            )

    loads[0].wait()
    for b in range(per_dev):
        loads[1 + b].wait()
        cols = slice(b * block_len, (b + 1) * block_len)
        forward[:, cols] = jnp.dot(
            rhs[:, cols], diag[b], preferred_element_type=F32
        ).astype(BF16)

    pl.semaphore_wait(barrier, count - 1)

    def index_copy(peer, slot, source):
        return pltpu.make_async_remote_copy(
            src_ref=index_ref.at[lax.rem(peer, tiles)],
            dst_ref=index_all.at[slot],
            send_sem=idx_send.at[peer],
            recv_sem=idx_recv.at[source],
            device_id=(peer // tiles, lax.rem(peer, tiles)),
            device_id_type=MESH,
        )

    def send_index(k, carry):
        index_copy(lax.rem(me + k, count), me, me).start()
        return carry

    lax.fori_loop(1, count, send_index, 0)
    own_index = pltpu.make_async_copy(index_ref.at[t], index_all.at[me], self_sem.at[0])
    own_index.start()

    def term_copy(pg, pt, source):
        return pltpu.make_async_remote_copy(
            src_ref=coupled.at[rows_of(pg), lanes(pt)],
            dst_ref=got.at[:, lanes(source)],
            send_sem=a_send.at[pg * tiles + pt],
            recv_sem=a_recv.at[source],
            device_id=(pg, pt),
            device_id_type=MESH,
        )

    for load in code_loads:
        load.wait()

    def couple(i, carry):
        q = lax.rem(t // chunk + 1 + i, chunks)
        code_rows = codes[pl.ds(pl.multiple_of(q * wide, wide), wide), :]
        terms = lax.dot_general(forward[...], code_rows, NT, preferred_element_type=F32)
        terms = terms * factor_ref[:, pl.ds(pl.multiple_of(q * wide, wide), wide)]
        coupled[:, pl.ds(pl.multiple_of(q * wide, wide), wide)] = terms.astype(BF16)

        def send(k, inner):
            pg = lax.rem(g + k // chunk, groups)
            pt = q * chunk + lax.rem(k, chunk)

            @pl.when(pg * tiles + pt != me)
            def _():
                term_copy(pg, pt, me).start()

            return inner

        return lax.fori_loop(0, groups * chunk, send, carry)

    lax.fori_loop(0, chunks, couple, 0)
    own_terms = pltpu.make_async_copy(
        coupled.at[rows_of(g), lanes(t)], got.at[:, lanes(me)], self_sem.at[1]
    )
    own_terms.start()

    own_index.wait()

    def index_done(k, carry):
        source = lax.rem(me + k, count)
        index_copy(source, source, source).wait_recv()
        return carry

    lax.fori_loop(1, count, index_done, 0)

    def select(source, carry):
        places = lax.broadcasted_iota(jnp.int32, (share, LANES), 0)
        onehot[:, lanes(source)] = jnp.where(places == index_all[source], 1.0, 0.0).astype(BF16)
        return carry

    lax.fori_loop(0, count, select, 0)

    own_terms.wait()

    def terms_done(k, carry):
        source = lax.rem(me + k, count)
        term_copy(source // tiles, lax.rem(source, tiles), source).wait_recv()
        return carry

    lax.fori_loop(1, count, terms_done, 0)
    own_share = lax.dot_general(got[...], onehot[...], NT, preferred_element_type=F32)
    residue = (rhs_sep_ref[rows_of(g), :].astype(F32) - own_share).astype(BF16)

    def part_copy(pt, source):
        return pltpu.make_async_remote_copy(
            src_ref=part.at[pt],
            dst_ref=part_got.at[source],
            send_sem=r_send.at[pt],
            recv_sem=r_recv.at[source],
            device_id=(g, pt),
            device_id_type=MESH,
        )

    root_load.wait()
    for c in range(tiles - 1, -1, -1):

        @pl.when(c >= t)
        def _():
            first = lane_window(c, share)
            part[c] = jnp.dot(
                residue, root[:, first : first + window], preferred_element_type=F32
            ).astype(BF16)

        @pl.when(c > t)
        def _():
            part_copy(c, t).start()

    def add_part(source, total):
        part_copy(source, source).wait_recv()
        return total + part_got[source].astype(F32)

    total = lax.fori_loop(0, t, add_part, part[t].astype(F32))
    offset = t * share - t * share // LANES * LANES
    column = lax.broadcasted_iota(jnp.int32, (rpg, window), 1)
    inside = jnp.logical_and(column >= offset, column < offset + share)
    fsep[t] = jnp.where(inside, total, 0.0).astype(BF16)

    def fsep_copy(pt, source):
        return pltpu.make_async_remote_copy(
            src_ref=fsep.at[source],
            dst_ref=fsep.at[source],
            send_sem=f_send.at[pt],
            recv_sem=f_recv.at[source],
            device_id=(g, pt),
            device_id_type=MESH,
        )

    def send_fsep(pt, carry):
        fsep_copy(pt, t).start()
        return carry

    lax.fori_loop(0, t, send_fsep, 0)
    solved[...] = jnp.zeros_like(solved)
    for c in range(tiles):

        @pl.when(c > t)
        def _():
            fsep_copy(c, c).wait_recv()

        @pl.when(c >= t)
        def _():
            first = lane_window(c, share)
            solved[...] += lax.dot_general(
                fsep[c], root[:, first : first + window], NT, preferred_element_type=F32
            )

    picked[...] = jnp.dot(
        solved[...].astype(BF16), onehot[...], preferred_element_type=F32
    ).astype(BF16)

    def pick_copy(peer, source):
        return pltpu.make_async_remote_copy(
            src_ref=picked.at[:, lanes(peer)],
            dst_ref=pick_got.at[rows_of(source // tiles), lanes(lax.rem(source, tiles))],
            send_sem=b_send.at[peer],
            recv_sem=b_recv.at[source],
            device_id=(peer // tiles, lax.rem(peer, tiles)),
            device_id_type=MESH,
        )

    def send_pick(k, carry):
        pick_copy(lax.rem(me + k, count), me).start()
        return carry

    lax.fori_loop(1, count, send_pick, 0)
    own_pick = pltpu.make_async_copy(
        picked.at[:, lanes(me)], pick_got.at[rows_of(g), lanes(t)], self_sem.at[2]
    )
    own_pick.start()

    def sep_copy(pg, source):
        return pltpu.make_async_remote_copy(
            src_ref=solved,
            dst_ref=sep_ref.at[rows_of(source)],
            send_sem=s_send.at[pg],
            recv_sem=s_recv.at[source],
            device_id=(pg, t),
            device_id_type=MESH,
        )

    def send_sep(k, carry):
        sep_copy(lax.rem(g + k, groups), g).start()
        return carry

    lax.fori_loop(1, groups, send_sep, 0)
    own_sep = pltpu.make_async_copy(solved, sep_ref.at[rows_of(g)], self_sem.at[3])
    own_sep.start()

    own_pick.wait()

    def pick_done(k, carry):
        source = lax.rem(me + k, count)
        pick_copy(source, source).wait_recv()
        return carry

    lax.fori_loop(1, count, pick_done, 0)
    weighted = (pick_got[...].astype(F32) * factor_ref[...]).astype(BF16)
    for b in range(per_dev):
        cols = slice(b * block_len, (b + 1) * block_len)
        update = jnp.dot(weighted, codes[:, cols], preferred_element_type=F32)
        misfit = (forward[:, cols].astype(F32) - update).astype(BF16)
        out_ref[:, cols] = lax.dot_general(
            misfit, diag[b], NT, preferred_element_type=F32
        ).astype(BF16)

    own_sep.wait()

    def sep_done(k, carry):
        source = lax.rem(g + k, groups)
        sep_copy(source, source).wait_recv()
        sep_copy(source, g).wait_send()
        return carry

    lax.fori_loop(1, groups, sep_done, 0)

    def sent(k, carry):
        peer = lax.rem(me + k, count)
        index_copy(peer, me, me).wait_send()
        term_copy(peer // tiles, lax.rem(peer, tiles), me).wait_send()
        pick_copy(peer, me).wait_send()
        return carry

    lax.fori_loop(1, count, sent, 0)

    def part_sent(pt, carry):
        part_copy(pt, t).wait_send()
        return carry

    lax.fori_loop(t + 1, tiles, part_sent, 0)

    def fsep_sent(pt, carry):
        fsep_copy(pt, t).wait_send()
        return carry

    lax.fori_loop(0, t, fsep_sent, 0)


def fused(rhs_local, diag_inv, codes, row_scales, sep_index, live_rows, rhs_sep, root_inv):
    rhs_count, local_len = rhs_local.shape
    per_dev, block_len = diag_inv.shape[0], diag_inv.shape[1]
    coupled_rows = codes.shape[0]
    share, sep_len = root_inv.shape
    groups, tiles = lax.axis_size("grid"), lax.axis_size("tile")
    count = groups * tiles
    per_share = coupled_rows // tiles
    rpg = rhs_count // groups
    window = share + (-share) % LANES
    pad = ((0, 0), (0, LANES - per_share))
    positions = jnp.arange(coupled_rows, dtype=jnp.int32)
    factor = row_scales * (positions < live_rows[0]).astype(F32)
    factor = jnp.pad(factor.reshape(tiles, per_share), pad).reshape(1, tiles * LANES)
    bases = (jnp.arange(tiles, dtype=jnp.int32) * share)[:, None]
    index = jnp.pad(
        sep_index.reshape(tiles, per_share) - bases, pad, constant_values=-1
    ).reshape(tiles, 1, LANES)
    vmem = pl.BlockSpec(memory_space=pltpu.VMEM)
    anywhere = pl.BlockSpec(memory_space=pl.ANY)
    dma = pltpu.SemaphoreType.DMA
    macs = rhs_count * local_len * 2 * (block_len + tiles * LANES)
    return pl.pallas_call(
        functools.partial(kernel, groups, tiles),
        out_shape=(
            jax.ShapeDtypeStruct((rhs_count, local_len), BF16),
            jax.ShapeDtypeStruct((rhs_count, share), F32),
        ),
        in_specs=[vmem, vmem, vmem, anywhere, anywhere, anywhere, anywhere],
        out_specs=(vmem, vmem),
        scratch_shapes=[
            pltpu.VMEM((rhs_count, local_len), BF16),
            pltpu.VMEM(diag_inv.shape, BF16),
            pltpu.VMEM((tiles * LANES, local_len), BF16),
            pltpu.VMEM(root_inv.shape, BF16),
            pltpu.VMEM((rhs_count, local_len), BF16),
            pltpu.VMEM((rhs_count, tiles * LANES), BF16),
            pltpu.VMEM((count, 1, LANES), jnp.int32),
            pltpu.VMEM((share, count * LANES), BF16),
            pltpu.VMEM((rpg, count * LANES), BF16),
            pltpu.VMEM((tiles, rpg, window), BF16),
            pltpu.VMEM((tiles, rpg, window), BF16),
            pltpu.VMEM((tiles, rpg, window), BF16),
            pltpu.VMEM((rpg, share), F32),
            pltpu.VMEM((rpg, count * LANES), BF16),
            pltpu.VMEM((rhs_count, tiles * LANES), BF16),
            dma((2 + per_dev,)),
            dma((tiles,)),
            dma((4,)),
            dma((count,)),
            dma((count,)),
            dma((count,)),
            dma((count,)),
            dma((tiles,)),
            dma((tiles,)),
            dma((tiles,)),
            dma((tiles,)),
            dma((groups,)),
            dma((groups,)),
            dma((count,)),
            dma((count,)),
        ],
        compiler_params=pltpu.CompilerParams(
            collective_id=0, has_side_effects=True, vmem_limit_bytes=48 * 1024 * 1024
        ),
        cost_estimate=pl.CostEstimate(
            flops=2 * macs,
            bytes_accessed=2 * (diag_inv.size + codes.size + root_inv.size + 2 * rhs_local.size),
            transcendentals=0,
        ),
    )(factor, index, rhs_sep, rhs_local, diag_inv, codes, root_inv)


def fits(mesh, rhs_local, diag_inv, codes, root_inv):
    groups, tiles = mesh.shape["grid"], mesh.shape["tile"]
    rhs_count = rhs_local.shape[0]
    per_share = codes.shape[0] // (groups * tiles) // tiles
    share = root_inv.shape[0] // tiles
    return (
        rhs_count % (groups * ROWS) == 0
        and tiles % 2 == 0
        and per_share % ROWS == 0
        and per_share <= LANES
        and share % (LANES // 2) == 0
        and diag_inv.shape[1] % LANES == 0
    )

def selector(offsets, share_len):
    columns = jnp.arange(share_len, dtype=jnp.int32)
    return (offsets[:, :, None] == columns[None, None, :]).astype(jnp.float32)


def on_device(rhs_local, diag_inv, codes, row_scales, sep_index, live_rows, rhs_sep, root_inv):
    rhs_count, local_len = rhs_local.shape
    per_dev, block_len = (diag_inv.shape[0], diag_inv.shape[1])
    coupled_rows = codes.shape[0]
    share_len, sep_len = root_inv.shape
    tile_count = lax.axis_size("tile")
    per_share = coupled_rows // tile_count
    pieces = []
    for block_pos in range(per_dev):
        columns = rhs_local[:, block_pos * block_len : (block_pos + 1) * block_len]
        pieces.append(jnp.dot(columns, diag_inv[block_pos], preferred_element_type=jnp.float32))
    forward_flat = jnp.concatenate(pieces, axis=1).astype(jnp.bfloat16)
    positions = jnp.arange(coupled_rows, dtype=jnp.int32)
    row_factor = row_scales * (positions < live_rows[0]).astype(jnp.float32)
    coupled = (
        lax.dot_general(
            forward_flat, codes, (((1,), (1,)), ((), ())), preferred_element_type=jnp.float32
        )
        * row_factor[None, :]
    )
    bases = (jnp.arange(tile_count, dtype=jnp.int32) * share_len)[:, None]
    local_offsets = sep_index.reshape(tile_count, per_share) - bases
    onehot = selector(local_offsets, share_len)
    values = coupled.reshape(rhs_count, tile_count, per_share)
    offsets = local_offsets.astype(jnp.float32)
    got_values, got_offsets = (
        lax.all_to_all(values, "tile", split_axis=1, concat_axis=1, tiled=True),
        lax.all_to_all(offsets[None], "tile", split_axis=1, concat_axis=1, tiled=True),
    )
    got_onehot = selector(got_offsets[0].astype(jnp.int32), share_len)
    own_share = jnp.einsum("rjp,jps->rs", got_values, got_onehot, precision=lax.Precision.HIGHEST)
    own_share = lax.psum(own_share, "grid")
    residue = (rhs_sep.astype(jnp.float32) - own_share).astype(jnp.bfloat16)
    root_part = jnp.dot(residue, root_inv, preferred_element_type=jnp.float32)
    forward_sep = lax.psum(root_part, "tile").astype(jnp.bfloat16)
    solved = lax.dot_general(
        forward_sep, root_inv, (((1,), (1,)), ((), ())), preferred_element_type=jnp.float32
    )
    gathered = lax.all_gather(solved.astype(jnp.bfloat16), "tile", axis=1, tiled=True)
    gathered_split = gathered.astype(jnp.float32).reshape(rhs_count, tile_count, share_len)
    picked = jnp.einsum(
        "rjs,jps->rjp", gathered_split, onehot, precision=lax.Precision.HIGHEST
    ).reshape(rhs_count, coupled_rows)
    weighted = (picked * row_factor[None, :]).astype(jnp.bfloat16)
    update = jnp.dot(weighted, codes, preferred_element_type=jnp.float32)
    misfit = (forward_flat.astype(jnp.float32) - update).astype(jnp.bfloat16)
    results = []
    for block_pos in range(per_dev):
        columns = misfit[:, block_pos * block_len : (block_pos + 1) * block_len]
        results.append(
            lax.dot_general(
                columns,
                diag_inv[block_pos],
                (((1,), (1,)), ((), ())),
                preferred_element_type=jnp.float32,
            )
        )
    result = jnp.concatenate(results, axis=1)
    return (result.astype(jnp.bfloat16), solved)


def solution(mesh):
    specs = (
        P(None, ("grid", "tile")),
        P(("grid", "tile"), None, None),
        P(("grid", "tile"), None),
        P(("grid", "tile")),
        P(("grid", "tile")),
        P(("grid", "tile")),
        P(None, "tile"),
        P("tile", None),
    )

    def run(*args):
        rhs_local, diag_inv, codes, root_inv = args[0], args[1], args[2], args[7]
        body = fused if fits(mesh, rhs_local, diag_inv, codes, root_inv) else on_device
        return jax.shard_map(
            body,
            mesh=mesh,
            in_specs=specs,
            out_specs=(P(None, ("grid", "tile")), P(None, "tile")),
            check_vma=False,
        )(*args)

    return run
```

```python
import functools

import jax
import jax.numpy as jnp
from jax import lax
from jax.experimental import pallas as pl
from jax.experimental.pallas import tpu as pltpu
from jax.sharding import PartitionSpec as P

LANES = 128
ROWS = 16
MESH = pl.DeviceIdType.MESH
F32 = jnp.float32
BF16 = jnp.bfloat16
NT = (((1,), (1,)), ((), ()))


def lane_index(rows):
    return lax.broadcasted_iota(jnp.int32, (rows, LANES), 1)


def pack(pieces, length):
    tiles = [None] * pl.cdiv(len(pieces) * length, LANES)
    lane = lane_index(pieces[0].shape[0])

    def add(tile, piece):
        tiles[tile] = piece if tiles[tile] is None else tiles[tile] + piece

    for pos, piece in enumerate(pieces):
        tile, shift = pos * length // LANES, pos * length % LANES
        turned = pltpu.roll(piece, shift, 1) if shift else piece
        if shift + length > LANES:
            add(tile, jnp.where(lane >= shift, turned, 0.0))
            add(tile + 1, jnp.where(lane < shift, turned, 0.0))
        else:
            add(tile, turned)
    return jnp.concatenate(tiles, axis=1)


def unpack(packed, pieces, length):
    lane = lane_index(packed.shape[0])
    out = []
    for pos in range(pieces):
        tile, shift = pos * length // LANES, pos * length % LANES
        piece = packed[:, tile * LANES : (tile + 1) * LANES]
        if shift:
            piece = pltpu.roll(piece, LANES - shift, 1)
        if shift + length > LANES:
            rest = packed[:, (tile + 1) * LANES : (tile + 2) * LANES]
            piece = jnp.where(lane < LANES - shift, piece, pltpu.roll(rest, LANES - shift, 1))
        out.append(piece)
    return out


def kernel(
    groups,
    tiles,
    factor_ref,
    index_ref,
    rhs_sep_ref,
    rhs_hbm,
    diag_hbm,
    codes_hbm,
    root_hbm,
    out_ref,
    sep_ref,
    rhs,
    diag,
    codes,
    root,
    forward,
    coupled,
    index_all,
    onehot,
    got,
    part,
    part_got,
    fsep,
    total,
    solved,
    picked,
    pick_got,
    update,
    load_sem,
    code_sem,
    self_sem,
    idx_send,
    idx_recv,
    a_send,
    a_recv,
    r_send,
    r_recv,
    f_send,
    f_recv,
    s_send,
    s_recv,
    b_send,
    b_recv,
):
    g = lax.axis_index("grid")
    t = lax.axis_index("tile")
    count = groups * tiles
    mine = t * groups + g
    per_dev, block_len = diag.shape[0], diag.shape[1]
    share = root.shape[0]
    per_share = codes_hbm.shape[0] // tiles
    rhs_count = rhs.shape[0]
    rpg = rhs_count // groups
    subs = rpg // ROWS
    span = groups * ROWS
    pairs = tiles // 2
    wide = 2 * LANES
    fan = 2 * groups
    pair_me = t // 2
    toward = 1 - 2 * (2 * pair_me // pairs)

    def pair_at(distance):
        return lax.rem(pair_me + toward * distance + pairs, pairs)

    def lanes(position, size=LANES):
        return pl.ds(pl.multiple_of(position * size, size), size)

    def rows_of(group):
        return pl.ds(pl.multiple_of(group * ROWS, ROWS), ROWS)

    def device(slot):
        return (lax.rem(slot, groups), slot // groups)

    barrier = pltpu.get_barrier_semaphore()

    def greet(k, carry):
        pl.semaphore_signal(
            barrier, inc=1, device_id=device(lax.rem(mine + k, count)), device_id_type=MESH
        )
        return carry

    lax.fori_loop(1, count, greet, 0)

    loads = [pltpu.make_async_copy(rhs_hbm, rhs, load_sem.at[0])]
    for b in range(per_dev):
        loads.append(pltpu.make_async_copy(diag_hbm.at[b], diag.at[b], load_sem.at[1 + b]))
    for load in loads:
        load.start()
    code_loads = []
    for j in range(tiles):
        code_loads.append(
            pltpu.make_async_copy(
                codes_hbm.at[pl.ds(j * per_share, per_share)],
                codes.at[pl.ds(j * LANES, per_share)],
                code_sem.at[j],
            )
        )
    for load in code_loads:
        load.start()
    root_load = pltpu.make_async_copy(root_hbm, root, load_sem.at[1 + per_dev])
    root_load.start()
    if per_share < LANES:
        for j in range(tiles):
            codes[j * LANES + per_share : (j + 1) * LANES, :] = jnp.zeros(
                (LANES - per_share, codes.shape[1]), BF16
            )

    loads[0].wait()
    for b in range(per_dev):
        loads[1 + b].wait()
        cols = slice(b * block_len, (b + 1) * block_len)
        forward[:, cols] = jnp.dot(
            rhs[:, cols], diag[b], preferred_element_type=F32
        ).astype(BF16)

    pl.semaphore_wait(barrier, count - 1)

    def index_copy(peer, source):
        return pltpu.make_async_remote_copy(
            src_ref=index_ref.at[peer // groups],
            dst_ref=index_all.at[source],
            send_sem=idx_send.at[peer],
            recv_sem=idx_recv.at[source],
            device_id=device(peer),
            device_id_type=MESH,
        )

    def send_index(k, carry):
        index_copy(lax.rem(mine + k, count), mine).start()
        return carry

    lax.fori_loop(1, count, send_index, 0)
    own_index = pltpu.make_async_copy(index_ref.at[t], index_all.at[mine], self_sem.at[0])
    own_index.start()

    def term_copy(peer, source):
        return pltpu.make_async_remote_copy(
            src_ref=coupled.at[peer // groups, rows_of(lax.rem(peer, groups))],
            dst_ref=got.at[source],
            send_sem=a_send.at[peer],
            recv_sem=a_recv.at[source],
            device_id=device(peer),
            device_id_type=MESH,
        )

    for load in code_loads:
        load.wait()

    def couple(i, carry):
        q = pair_at(pairs - 1 - i)
        terms = lax.dot_general(
            forward[...], codes[lanes(q, wide), :], NT, preferred_element_type=F32
        )
        terms = terms * factor_ref[:, lanes(q, wide)]
        for u in range(2):
            ours = terms[:, u * LANES : (u + 1) * LANES]
            pieces = [ours[j * span : (j + 1) * span] for j in range(subs)]
            coupled[2 * q + u] = pack(pieces, per_share).astype(BF16)

        def send(k, inner):
            peer = q * fan + k

            @pl.when(peer != mine)
            def _():
                term_copy(peer, mine).start()

            return inner

        return lax.fori_loop(0, fan, send, carry)

    lax.fori_loop(0, pairs, couple, 0)
    own_terms = pltpu.make_async_copy(coupled.at[t, rows_of(g)], got.at[mine], self_sem.at[1])
    own_terms.start()

    own_index.wait()

    def index_done(k, carry):
        source = lax.rem(mine + k, count)
        index_copy(source, source).wait_recv()
        return carry

    lax.fori_loop(1, count, index_done, 0)

    def select(source, carry):
        places = lax.broadcasted_iota(jnp.int32, (share, LANES), 0)
        onehot[:, lanes(source)] = jnp.where(places == index_all[source], 1.0, 0.0).astype(BF16)
        return carry

    lax.fori_loop(0, count, select, 0)

    own_terms.wait()
    total[...] = jnp.zeros_like(total)

    def gather_terms(i, carry):
        q = pair_at(i)

        def arrived(k, inner):
            source = q * fan + k

            @pl.when(source != mine)
            def _():
                term_copy(source, source).wait_recv()

            return inner

        lax.fori_loop(0, fan, arrived, 0)
        columns = []
        for k in range(fan):
            pieces = unpack(got[q * fan + k].astype(F32), subs, per_share)
            columns.append(jnp.concatenate(pieces, axis=0).astype(BF16))
        total[...] += lax.dot_general(
            jnp.concatenate(columns, axis=1),
            onehot[:, lanes(q, fan * LANES)],
            NT,
            preferred_element_type=F32,
        )
        return carry

    lax.fori_loop(0, pairs, gather_terms, 0)
    rhs_sep = jnp.concatenate(
        [
            rhs_sep_ref[pl.ds(pl.multiple_of(j * span + g * ROWS, ROWS), ROWS), :]
            for j in range(subs)
        ],
        axis=0,
    )
    residue = (rhs_sep.astype(F32) - total[...]).astype(BF16)

    def owner_of(pair):
        return max(pair - 1, 0) * 2 + lax.rem(g, 2)

    def part_copy(pair, source):
        return pltpu.make_async_remote_copy(
            src_ref=part.at[pair],
            dst_ref=part_got.at[pair, source],
            send_sem=r_send.at[pair],
            recv_sem=r_recv.at[pair, source],
            device_id=(g, owner_of(pair)),
            device_id_type=MESH,
        )

    def block(pair):
        return slice(pair * 2 * share, (pair + 1) * 2 * share)

    root_load.wait()
    for pair in range(pairs - 1, -1, -1):

        @pl.when(t < 2 * pair + 2)
        def _():
            part[pair] = jnp.dot(
                residue, root[:, block(pair)], preferred_element_type=F32
            ).astype(BF16)

            @pl.when(t != owner_of(pair))
            def _():
                part_copy(pair, t).start()

    def fsep_copy(pair, peer):
        return pltpu.make_async_remote_copy(
            src_ref=fsep.at[pair],
            dst_ref=fsep.at[pair],
            send_sem=f_send.at[pair, peer],
            recv_sem=f_recv.at[pair],
            device_id=(g, peer),
            device_id_type=MESH,
        )

    for pair in range(pairs):

        @pl.when(t == owner_of(pair))
        def _():
            def add_part(k, summed):
                source = lax.rem(t + k, 2 * pair + 2)
                part_copy(pair, source).wait_recv()
                return summed + part_got[pair, source].astype(F32)

            summed = lax.fori_loop(1, 2 * pair + 2, add_part, part[pair].astype(F32))
            fsep[pair] = summed.astype(BF16)

            def send_fsep(k, carry):
                fsep_copy(pair, lax.rem(t + k, 2 * pair + 2)).start()
                return carry

            lax.fori_loop(1, 2 * pair + 2, send_fsep, 0)

    total[...] = jnp.zeros_like(total)
    for pair in range(pairs):

        @pl.when(t < 2 * pair + 2)
        def _():
            @pl.when(t != owner_of(pair))
            def _():
                fsep_copy(pair, t).wait_recv()

            total[...] += lax.dot_general(
                fsep[pair], root[:, block(pair)], NT, preferred_element_type=F32
            )

    for j in range(subs):
        solved[j] = total[j * ROWS : (j + 1) * ROWS, :]
    rounded = total[...].astype(BF16)

    def pick_copy(peer, source):
        return pltpu.make_async_remote_copy(
            src_ref=picked.at[peer],
            dst_ref=pick_got.at[source // groups, rows_of(lax.rem(source, groups))],
            send_sem=b_send.at[peer],
            recv_sem=b_recv.at[source],
            device_id=device(peer),
            device_id_type=MESH,
        )

    def pick(i, carry):
        q = pair_at(pairs - 1 - i)
        found = jnp.dot(rounded, onehot[:, lanes(q, fan * LANES)], preferred_element_type=F32)
        for k in range(fan):
            ours = found[:, k * LANES : (k + 1) * LANES]
            pieces = [ours[j * ROWS : (j + 1) * ROWS] for j in range(subs)]
            picked[q * fan + k] = pack(pieces, per_share).astype(BF16)

        def send(k, inner):
            peer = q * fan + k

            @pl.when(peer != mine)
            def _():
                pick_copy(peer, mine).start()

            return inner

        return lax.fori_loop(0, fan, send, carry)

    lax.fori_loop(0, pairs, pick, 0)
    own_pick = pltpu.make_async_copy(picked.at[mine], pick_got.at[t, rows_of(g)], self_sem.at[2])
    own_pick.start()

    def sep_copy(pg, source):
        return pltpu.make_async_remote_copy(
            src_ref=solved,
            dst_ref=sep_ref.at[:, rows_of(source)],
            send_sem=s_send.at[pg],
            recv_sem=s_recv.at[source],
            device_id=(pg, t),
            device_id_type=MESH,
        )

    def send_sep(k, carry):
        sep_copy(lax.rem(g + k, groups), g).start()
        return carry

    lax.fori_loop(1, groups, send_sep, 0)
    own_sep = pltpu.make_async_copy(solved, sep_ref.at[:, rows_of(g)], self_sem.at[3])
    own_sep.start()

    own_pick.wait()
    update[...] = jnp.zeros_like(update)

    def gather_picks(i, carry):
        q = pair_at(i)

        def arrived(k, inner):
            source = q * fan + k

            @pl.when(source != mine)
            def _():
                pick_copy(source, source).wait_recv()

            return inner

        lax.fori_loop(0, fan, arrived, 0)
        columns = []
        for u in range(2):
            pieces = unpack(pick_got[2 * q + u].astype(F32), subs, per_share)
            columns.append(jnp.concatenate(pieces, axis=0))
        weighted = jnp.concatenate(columns, axis=1) * factor_ref[:, lanes(q, wide)]
        update[...] += jnp.dot(
            weighted.astype(BF16), codes[lanes(q, wide), :], preferred_element_type=F32
        )
        return carry

    lax.fori_loop(0, pairs, gather_picks, 0)
    for b in range(per_dev):
        cols = slice(b * block_len, (b + 1) * block_len)
        misfit = (forward[:, cols].astype(F32) - update[:, cols]).astype(BF16)
        out_ref[:, cols] = lax.dot_general(
            misfit, diag[b], NT, preferred_element_type=F32
        ).astype(BF16)

    own_sep.wait()

    def sep_done(k, carry):
        source = lax.rem(g + k, groups)
        sep_copy(source, source).wait_recv()
        sep_copy(source, g).wait_send()
        return carry

    lax.fori_loop(1, groups, sep_done, 0)

    def sent(k, carry):
        peer = lax.rem(mine + k, count)
        index_copy(peer, mine).wait_send()
        term_copy(peer, mine).wait_send()
        pick_copy(peer, mine).wait_send()
        return carry

    lax.fori_loop(1, count, sent, 0)
    for pair in range(pairs):

        @pl.when(jnp.logical_and(t < 2 * pair + 2, t != owner_of(pair)))
        def _():
            part_copy(pair, t).wait_send()

        @pl.when(t == owner_of(pair))
        def _():
            def fsep_sent(k, carry):
                fsep_copy(pair, lax.rem(t + k, 2 * pair + 2)).wait_send()
                return carry

            lax.fori_loop(1, 2 * pair + 2, fsep_sent, 0)


def fused(rhs_local, diag_inv, codes, row_scales, sep_index, live_rows, rhs_sep, root_inv):
    rhs_count, local_len = rhs_local.shape
    per_dev, block_len = diag_inv.shape[0], diag_inv.shape[1]
    coupled_rows = codes.shape[0]
    share, sep_len = root_inv.shape
    groups, tiles = lax.axis_size("grid"), lax.axis_size("tile")
    count = groups * tiles
    per_share = coupled_rows // tiles
    rpg = rhs_count // groups
    subs, pairs = rpg // ROWS, tiles // 2
    packed = pl.cdiv(subs * per_share, LANES) * LANES
    pad = ((0, 0), (0, LANES - per_share))
    positions = jnp.arange(coupled_rows, dtype=jnp.int32)
    factor = row_scales * (positions < live_rows[0]).astype(F32)
    factor = jnp.pad(factor.reshape(tiles, per_share), pad).reshape(1, tiles * LANES)
    bases = (jnp.arange(tiles, dtype=jnp.int32) * share)[:, None]
    index = jnp.pad(
        sep_index.reshape(tiles, per_share) - bases, pad, constant_values=-1
    ).reshape(tiles, 1, LANES)
    vmem = pl.BlockSpec(memory_space=pltpu.VMEM)
    anywhere = pl.BlockSpec(memory_space=pl.ANY)
    dma = pltpu.SemaphoreType.DMA
    macs = rhs_count * local_len * 2 * (block_len + tiles * LANES)
    local, sep = pl.pallas_call(
        functools.partial(kernel, groups, tiles),
        out_shape=(
            jax.ShapeDtypeStruct((rhs_count, local_len), BF16),
            jax.ShapeDtypeStruct((subs, groups * ROWS, share), F32),
        ),
        in_specs=[vmem, vmem, vmem, anywhere, anywhere, anywhere, anywhere],
        out_specs=(vmem, vmem),
        scratch_shapes=[
            pltpu.VMEM((rhs_count, local_len), BF16),
            pltpu.VMEM(diag_inv.shape, BF16),
            pltpu.VMEM((tiles * LANES, local_len), BF16),
            pltpu.VMEM(root_inv.shape, BF16),
            pltpu.VMEM((rhs_count, local_len), BF16),
            pltpu.VMEM((tiles, groups * ROWS, packed), BF16),
            pltpu.VMEM((count, 1, LANES), jnp.int32),
            pltpu.VMEM((share, count * LANES), BF16),
            pltpu.VMEM((count, ROWS, packed), BF16),
            pltpu.VMEM((pairs, rpg, 2 * share), BF16),
            pltpu.VMEM((pairs, tiles, rpg, 2 * share), BF16),
            pltpu.VMEM((pairs, rpg, 2 * share), BF16),
            pltpu.VMEM((rpg, share), F32),
            pltpu.VMEM((subs, ROWS, share), F32),
            pltpu.VMEM((count, ROWS, packed), BF16),
            pltpu.VMEM((tiles, groups * ROWS, packed), BF16),
            pltpu.VMEM((rhs_count, local_len), F32),
            dma((2 + per_dev,)),
            dma((tiles,)),
            dma((4,)),
            dma((count,)),
            dma((count,)),
            dma((count,)),
            dma((count,)),
            dma((pairs,)),
            dma((pairs, tiles)),
            dma((pairs, tiles)),
            dma((pairs,)),
            dma((groups,)),
            dma((groups,)),
            dma((count,)),
            dma((count,)),
        ],
        compiler_params=pltpu.CompilerParams(
            collective_id=0, has_side_effects=True, vmem_limit_bytes=60 * 1024 * 1024
        ),
        cost_estimate=pl.CostEstimate(
            flops=2 * macs,
            bytes_accessed=2 * (diag_inv.size + codes.size + root_inv.size + 2 * rhs_local.size),
            transcendentals=0,
        ),
    )(factor, index, rhs_sep, rhs_local, diag_inv, codes, root_inv)
    return local, sep.reshape(rhs_count, share)


def fits(mesh, rhs_local, diag_inv, codes, root_inv):
    groups, tiles = mesh.shape["grid"], mesh.shape["tile"]
    rhs_count = rhs_local.shape[0]
    per_share = codes.shape[0] // (groups * tiles) // tiles
    share = root_inv.shape[0] // tiles
    return (
        rhs_count % (groups * ROWS) == 0
        and tiles % 2 == 0
        and per_share % ROWS == 0
        and per_share <= LANES
        and share % (LANES // 2) == 0
        and diag_inv.shape[1] % LANES == 0
    )

def selector(offsets, share_len):
    columns = jnp.arange(share_len, dtype=jnp.int32)
    return (offsets[:, :, None] == columns[None, None, :]).astype(jnp.float32)


def on_device(rhs_local, diag_inv, codes, row_scales, sep_index, live_rows, rhs_sep, root_inv):
    rhs_count, local_len = rhs_local.shape
    per_dev, block_len = (diag_inv.shape[0], diag_inv.shape[1])
    coupled_rows = codes.shape[0]
    share_len, sep_len = root_inv.shape
    tile_count = lax.axis_size("tile")
    per_share = coupled_rows // tile_count
    pieces = []
    for block_pos in range(per_dev):
        columns = rhs_local[:, block_pos * block_len : (block_pos + 1) * block_len]
        pieces.append(jnp.dot(columns, diag_inv[block_pos], preferred_element_type=jnp.float32))
    forward_flat = jnp.concatenate(pieces, axis=1).astype(jnp.bfloat16)
    positions = jnp.arange(coupled_rows, dtype=jnp.int32)
    row_factor = row_scales * (positions < live_rows[0]).astype(jnp.float32)
    coupled = (
        lax.dot_general(
            forward_flat, codes, (((1,), (1,)), ((), ())), preferred_element_type=jnp.float32
        )
        * row_factor[None, :]
    )
    bases = (jnp.arange(tile_count, dtype=jnp.int32) * share_len)[:, None]
    local_offsets = sep_index.reshape(tile_count, per_share) - bases
    onehot = selector(local_offsets, share_len)
    values = coupled.reshape(rhs_count, tile_count, per_share)
    offsets = local_offsets.astype(jnp.float32)
    got_values, got_offsets = (
        lax.all_to_all(values, "tile", split_axis=1, concat_axis=1, tiled=True),
        lax.all_to_all(offsets[None], "tile", split_axis=1, concat_axis=1, tiled=True),
    )
    got_onehot = selector(got_offsets[0].astype(jnp.int32), share_len)
    own_share = jnp.einsum("rjp,jps->rs", got_values, got_onehot, precision=lax.Precision.HIGHEST)
    own_share = lax.psum(own_share, "grid")
    residue = (rhs_sep.astype(jnp.float32) - own_share).astype(jnp.bfloat16)
    root_part = jnp.dot(residue, root_inv, preferred_element_type=jnp.float32)
    forward_sep = lax.psum(root_part, "tile").astype(jnp.bfloat16)
    solved = lax.dot_general(
        forward_sep, root_inv, (((1,), (1,)), ((), ())), preferred_element_type=jnp.float32
    )
    gathered = lax.all_gather(solved.astype(jnp.bfloat16), "tile", axis=1, tiled=True)
    gathered_split = gathered.astype(jnp.float32).reshape(rhs_count, tile_count, share_len)
    picked = jnp.einsum(
        "rjs,jps->rjp", gathered_split, onehot, precision=lax.Precision.HIGHEST
    ).reshape(rhs_count, coupled_rows)
    weighted = (picked * row_factor[None, :]).astype(jnp.bfloat16)
    update = jnp.dot(weighted, codes, preferred_element_type=jnp.float32)
    misfit = (forward_flat.astype(jnp.float32) - update).astype(jnp.bfloat16)
    results = []
    for block_pos in range(per_dev):
        columns = misfit[:, block_pos * block_len : (block_pos + 1) * block_len]
        results.append(
            lax.dot_general(
                columns,
                diag_inv[block_pos],
                (((1,), (1,)), ((), ())),
                preferred_element_type=jnp.float32,
            )
        )
    result = jnp.concatenate(results, axis=1)
    return (result.astype(jnp.bfloat16), solved)


def solution(mesh):
    specs = (
        P(None, ("grid", "tile")),
        P(("grid", "tile"), None, None),
        P(("grid", "tile"), None),
        P(("grid", "tile")),
        P(("grid", "tile")),
        P(("grid", "tile")),
        P(None, "tile"),
        P("tile", None),
    )

    def run(*args):
        rhs_local, diag_inv, codes, root_inv = args[0], args[1], args[2], args[7]
        body = fused if fits(mesh, rhs_local, diag_inv, codes, root_inv) else on_device
        return jax.shard_map(
            body,
            mesh=mesh,
            in_specs=specs,
            out_specs=(P(None, ("grid", "tile")), P(None, "tile")),
            check_vma=False,
        )(*args)

    return run
```

```python
import functools

import jax
import jax.numpy as jnp
from jax import lax
from jax.experimental import pallas as pl
from jax.experimental.pallas import tpu as pltpu
from jax.sharding import PartitionSpec as P

LANES = 128
ROWS = 16
VMEM_BYTES = 54 * 1024 * 1024
MESH = pl.DeviceIdType.MESH
F32 = jnp.float32
BF16 = jnp.bfloat16
NT = (((1,), (1,)), ((), ()))


def lane_index(rows):
    return lax.broadcasted_iota(jnp.int32, (rows, LANES), 1)


def pack(pieces, length):
    tiles = [None] * pl.cdiv(len(pieces) * length, LANES)
    lane = lane_index(pieces[0].shape[0])

    def add(tile, piece):
        tiles[tile] = piece if tiles[tile] is None else tiles[tile] + piece

    for pos, piece in enumerate(pieces):
        tile, shift = pos * length // LANES, pos * length % LANES
        turned = pltpu.roll(piece, shift, 1) if shift else piece
        if shift + length > LANES:
            add(tile, jnp.where(lane >= shift, turned, 0.0))
            add(tile + 1, jnp.where(lane < shift, turned, 0.0))
        else:
            add(tile, turned)
    return jnp.concatenate(tiles, axis=1)


def unpack(packed, pieces, length):
    lane = lane_index(packed.shape[0])
    out = []
    for pos in range(pieces):
        tile, shift = pos * length // LANES, pos * length % LANES
        piece = packed[:, tile * LANES : (tile + 1) * LANES]
        if shift:
            piece = pltpu.roll(piece, LANES - shift, 1)
        if shift + length > LANES:
            rest = packed[:, (tile + 1) * LANES : (tile + 2) * LANES]
            piece = jnp.where(lane < LANES - shift, piece, pltpu.roll(rest, LANES - shift, 1))
        out.append(piece)
    return out


def kernel(
    groups,
    tiles,
    live_ref,
    scales_ref,
    places_ref,
    rhs_sep_ref,
    rhs_hbm,
    diag_hbm,
    codes_hbm,
    root_hbm,
    out_hbm,
    sep_hbm,
    rhs,
    diag,
    codes,
    root,
    forward,
    coupled,
    index_all,
    onehot,
    got,
    part,
    part_got,
    fsep,
    total,
    solved,
    picked,
    pick_got,
    update,
    factor_ref,
    index_ref,
    out_ref,
    sep_ref,
    store_sem,
    load_sem,
    code_sem,
    self_sem,
    idx_send,
    idx_recv,
    a_send,
    a_recv,
    r_send,
    r_recv,
    f_send,
    f_recv,
    s_send,
    s_recv,
    b_send,
    b_recv,
):
    g = lax.axis_index("grid")
    t = lax.axis_index("tile")
    count = groups * tiles
    mine = t * groups + g
    per_dev, block_len = diag.shape[0], diag.shape[1]
    share = root.shape[0]
    per_share = codes_hbm.shape[0] // tiles
    rhs_count = rhs.shape[0]
    rpg = rhs_count // groups
    subs = rpg // ROWS
    span = groups * ROWS
    pairs = tiles // 2
    wide = 2 * LANES
    fan = 2 * groups
    pair_me = t // 2
    toward = 1 - 2 * (2 * pair_me // pairs)

    def pair_at(distance):
        return lax.rem(pair_me + toward * distance + pairs, pairs)

    def lanes(position, size=LANES):
        return pl.ds(pl.multiple_of(position * size, size), size)

    def rows_of(group):
        return pl.ds(pl.multiple_of(group * ROWS, ROWS), ROWS)

    def halves(b):
        half = block_len // 2
        return [(b * block_len + h * half, b * block_len + (h + 1) * half) for h in range(2)]

    def device(slot):
        return (lax.rem(slot, groups), slot // groups)

    barrier = pltpu.get_barrier_semaphore()

    def greet(k, carry):
        pl.semaphore_signal(
            barrier, inc=1, device_id=device(lax.rem(mine + k, count)), device_id_type=MESH
        )
        return carry

    lax.fori_loop(1, count, greet, 0)

    loads = [pltpu.make_async_copy(rhs_hbm, rhs, load_sem.at[0])]
    for b in range(per_dev):
        loads.append(pltpu.make_async_copy(diag_hbm.at[b], diag.at[b], load_sem.at[1 + b]))
    for load in loads:
        load.start()
    code_loads = []
    for j in range(tiles):
        code_loads.append(
            pltpu.make_async_copy(
                codes_hbm.at[pl.ds(j * per_share, per_share)],
                codes.at[pl.ds(j * LANES, per_share)],
                code_sem.at[j],
            )
        )
    for load in code_loads:
        load.start()
    root_load = pltpu.make_async_copy(root_hbm, root, load_sem.at[1 + per_dev])
    root_load.start()
    if per_share < LANES:
        for j in range(tiles):
            codes[j * LANES + per_share : (j + 1) * LANES, :] = jnp.zeros(
                (LANES - per_share, codes.shape[1]), BF16
            )

    all_rows = scales_ref.shape[0]
    eight = (8, all_rows)
    scales = jnp.broadcast_to(scales_ref[...][None, :], eight)
    places = jnp.broadcast_to(places_ref[...][None, :], eight)
    position = lax.broadcasted_iota(jnp.int32, eight, 1)
    scales = jnp.where(position < live_ref[0], scales, 0.0)
    filled = lane_index(8) < per_share
    for j in range(tiles):
        shift = (all_rows - j * per_share) % all_rows
        turned = [pltpu.roll(x, shift, 1) if shift else x for x in (scales, places)]
        factor_ref[:, j * LANES : (j + 1) * LANES] = jnp.where(filled, turned[0][:, :LANES], 0.0)[:1]
        index_ref[j] = jnp.where(filled, turned[1][:, :LANES] - j * share, -1)[:1]

    loads[0].wait()
    for b in range(per_dev):
        loads[1 + b].wait()
        for low, high in halves(b):
            forward[:, low:high] = jnp.dot(
                rhs[:, b * block_len : high],
                diag[b, : high - b * block_len, low - b * block_len : high - b * block_len],
                preferred_element_type=F32,
            ).astype(BF16)

    pl.semaphore_wait(barrier, count - 1)

    def index_copy(peer, source):
        return pltpu.make_async_remote_copy(
            src_ref=index_ref.at[peer // groups],
            dst_ref=index_all.at[source],
            send_sem=idx_send.at[peer],
            recv_sem=idx_recv.at[source],
            device_id=device(peer),
            device_id_type=MESH,
        )

    def send_index(k, carry):
        index_copy(lax.rem(mine + k, count), mine).start()
        return carry

    lax.fori_loop(1, count, send_index, 0)
    own_index = pltpu.make_async_copy(index_ref.at[t], index_all.at[mine], self_sem.at[0])
    own_index.start()

    def term_copy(peer, source):
        return pltpu.make_async_remote_copy(
            src_ref=coupled.at[peer // groups, rows_of(lax.rem(peer, groups))],
            dst_ref=got.at[source],
            send_sem=a_send.at[peer],
            recv_sem=a_recv.at[source],
            device_id=device(peer),
            device_id_type=MESH,
        )

    for load in code_loads:
        load.wait()

    def couple(i, carry):
        q = pair_at(pairs - 1 - i)
        terms = lax.dot_general(
            forward[...], codes[lanes(q, wide), :], NT, preferred_element_type=F32
        )
        terms = terms * factor_ref[:, lanes(q, wide)]
        for u in range(2):
            ours = terms[:, u * LANES : (u + 1) * LANES]
            pieces = [ours[j * span : (j + 1) * span] for j in range(subs)]
            coupled[2 * q + u] = pack(pieces, per_share).astype(BF16)

        def send(k, inner):
            peer = q * fan + k

            @pl.when(peer != mine)
            def _():
                term_copy(peer, mine).start()

            return inner

        return lax.fori_loop(0, fan, send, carry)

    lax.fori_loop(0, pairs, couple, 0)
    own_terms = pltpu.make_async_copy(coupled.at[t, rows_of(g)], got.at[mine], self_sem.at[1])
    own_terms.start()

    own_index.wait()

    def index_done(k, carry):
        source = lax.rem(mine + k, count)
        index_copy(source, source).wait_recv()
        return carry

    lax.fori_loop(1, count, index_done, 0)

    def select(source, carry):
        places = lax.broadcasted_iota(jnp.int32, (share, LANES), 0)
        onehot[:, lanes(source)] = jnp.where(places == index_all[source], 1.0, 0.0).astype(BF16)
        return carry

    lax.fori_loop(0, count, select, 0)

    own_terms.wait()
    total[...] = jnp.zeros_like(total)

    def gather_terms(i, carry):
        q = pair_at(i)

        def arrived(k, inner):
            source = q * fan + k

            @pl.when(source != mine)
            def _():
                term_copy(source, source).wait_recv()

            return inner

        lax.fori_loop(0, fan, arrived, 0)
        columns = []
        for k in range(fan):
            pieces = unpack(got[q * fan + k].astype(F32), subs, per_share)
            columns.append(jnp.concatenate(pieces, axis=0).astype(BF16))
        total[...] += lax.dot_general(
            jnp.concatenate(columns, axis=1),
            onehot[:, lanes(q, fan * LANES)],
            NT,
            preferred_element_type=F32,
        )
        return carry

    lax.fori_loop(0, pairs, gather_terms, 0)
    rhs_sep = jnp.concatenate(
        [
            rhs_sep_ref[pl.ds(pl.multiple_of(j * span + g * ROWS, ROWS), ROWS), :]
            for j in range(subs)
        ],
        axis=0,
    )
    residue = (rhs_sep.astype(F32) - total[...]).astype(BF16)

    def owner_of(pair):
        return max(pair - 1, 0) * 2 + lax.rem(g, 2)

    def part_copy(pair, source):
        return pltpu.make_async_remote_copy(
            src_ref=part.at[pair],
            dst_ref=part_got.at[pair, source],
            send_sem=r_send.at[pair],
            recv_sem=r_recv.at[pair, source],
            device_id=(g, owner_of(pair)),
            device_id_type=MESH,
        )

    def block(pair):
        return slice(pair * 2 * share, (pair + 1) * 2 * share)

    root_load.wait()
    for pair in range(pairs - 1, -1, -1):

        @pl.when(t < 2 * pair + 2)
        def _():
            part[pair] = jnp.dot(
                residue, root[:, block(pair)], preferred_element_type=F32
            ).astype(BF16)

            @pl.when(t != owner_of(pair))
            def _():
                part_copy(pair, t).start()

    def fsep_copy(pair, peer):
        return pltpu.make_async_remote_copy(
            src_ref=fsep.at[pair],
            dst_ref=fsep.at[pair],
            send_sem=f_send.at[pair, peer],
            recv_sem=f_recv.at[pair],
            device_id=(g, peer),
            device_id_type=MESH,
        )

    for pair in range(pairs):

        @pl.when(t == owner_of(pair))
        def _():
            def add_part(k, summed):
                source = lax.rem(t + k, 2 * pair + 2)
                part_copy(pair, source).wait_recv()
                return summed + part_got[pair, source].astype(F32)

            summed = lax.fori_loop(1, 2 * pair + 2, add_part, part[pair].astype(F32))
            fsep[pair] = summed.astype(BF16)

            def send_fsep(k, carry):
                fsep_copy(pair, lax.rem(t + k, 2 * pair + 2)).start()
                return carry

            lax.fori_loop(1, 2 * pair + 2, send_fsep, 0)

    total[...] = jnp.zeros_like(total)
    for pair in range(pairs):

        @pl.when(t < 2 * pair + 2)
        def _():
            @pl.when(t != owner_of(pair))
            def _():
                fsep_copy(pair, t).wait_recv()

            total[...] += lax.dot_general(
                fsep[pair], root[:, block(pair)], NT, preferred_element_type=F32
            )

    for j in range(subs):
        solved[j] = total[j * ROWS : (j + 1) * ROWS, :]
    rounded = total[...].astype(BF16)

    def pick_copy(peer, source):
        return pltpu.make_async_remote_copy(
            src_ref=picked.at[peer],
            dst_ref=pick_got.at[source // groups, rows_of(lax.rem(source, groups))],
            send_sem=b_send.at[peer],
            recv_sem=b_recv.at[source],
            device_id=device(peer),
            device_id_type=MESH,
        )

    def pick(i, carry):
        q = pair_at(pairs - 1 - i)
        found = jnp.dot(rounded, onehot[:, lanes(q, fan * LANES)], preferred_element_type=F32)
        for k in range(fan):
            ours = found[:, k * LANES : (k + 1) * LANES]
            pieces = [ours[j * ROWS : (j + 1) * ROWS] for j in range(subs)]
            picked[q * fan + k] = pack(pieces, per_share).astype(BF16)

        def send(k, inner):
            peer = q * fan + k

            @pl.when(peer != mine)
            def _():
                pick_copy(peer, mine).start()

            return inner

        return lax.fori_loop(0, fan, send, carry)

    lax.fori_loop(0, pairs, pick, 0)
    own_pick = pltpu.make_async_copy(picked.at[mine], pick_got.at[t, rows_of(g)], self_sem.at[2])
    own_pick.start()

    def sep_copy(pg, source):
        return pltpu.make_async_remote_copy(
            src_ref=solved,
            dst_ref=sep_ref.at[:, rows_of(source)],
            send_sem=s_send.at[pg],
            recv_sem=s_recv.at[source],
            device_id=(pg, t),
            device_id_type=MESH,
        )

    def send_sep(k, carry):
        sep_copy(lax.rem(g + k, groups), g).start()
        return carry

    lax.fori_loop(1, groups, send_sep, 0)
    own_sep = pltpu.make_async_copy(solved, sep_ref.at[:, rows_of(g)], self_sem.at[3])
    own_sep.start()

    own_pick.wait()
    update[...] = jnp.zeros_like(update)

    def gather_picks(i, carry):
        q = pair_at(i)

        def arrived(k, inner):
            source = q * fan + k

            @pl.when(source != mine)
            def _():
                pick_copy(source, source).wait_recv()

            return inner

        lax.fori_loop(0, fan, arrived, 0)
        columns = []
        for u in range(2):
            pieces = unpack(pick_got[2 * q + u].astype(F32), subs, per_share)
            columns.append(jnp.concatenate(pieces, axis=0))
        weighted = jnp.concatenate(columns, axis=1) * factor_ref[:, lanes(q, wide)]
        update[...] += jnp.dot(
            weighted.astype(BF16), codes[lanes(q, wide), :], preferred_element_type=F32
        )
        return carry

    lax.fori_loop(0, pairs, gather_picks, 0)
    own_sep.wait()

    def sep_done(k, carry):
        source = lax.rem(g + k, groups)
        sep_copy(source, source).wait_recv()
        sep_copy(source, g).wait_send()
        return carry

    lax.fori_loop(1, groups, sep_done, 0)

    stores = [pltpu.make_async_copy(sep_ref, sep_hbm, store_sem.at[per_dev])]
    stores[0].start()
    for b in range(per_dev):
        cols = slice(b * block_len, (b + 1) * block_len)
        misfit = (forward[:, cols].astype(F32) - update[:, cols]).astype(BF16)
        for low, high in halves(b):
            first = low - b * block_len
            out_ref[:, low:high] = lax.dot_general(
                misfit[:, first:],
                diag[b, first : high - b * block_len, first:],
                NT,
                preferred_element_type=F32,
            ).astype(BF16)
        stores.append(
            pltpu.make_async_copy(out_ref.at[:, cols], out_hbm.at[:, cols], store_sem.at[b])
        )
        stores[-1].start()

    def sent(k, carry):
        peer = lax.rem(mine + k, count)
        index_copy(peer, mine).wait_send()
        term_copy(peer, mine).wait_send()
        pick_copy(peer, mine).wait_send()
        return carry

    lax.fori_loop(1, count, sent, 0)
    for pair in range(pairs):

        @pl.when(jnp.logical_and(t < 2 * pair + 2, t != owner_of(pair)))
        def _():
            part_copy(pair, t).wait_send()

        @pl.when(t == owner_of(pair))
        def _():
            def fsep_sent(k, carry):
                fsep_copy(pair, lax.rem(t + k, 2 * pair + 2)).wait_send()
                return carry

            lax.fori_loop(1, 2 * pair + 2, fsep_sent, 0)

    for store in stores:
        store.wait()


def hand_over(local_in, sep_in, local_out, sep_out, sems):
    parts = sems.shape[0] // 2
    copies = []
    for source, dest in ((local_in, local_out), (sep_in, sep_out)):
        rows = source.shape[0] // parts
        for part in range(parts):
            these = pl.ds(part * rows, rows)
            copies.append(
                pltpu.make_async_copy(source.at[these], dest.at[these], sems.at[len(copies)])
            )
    for copy in copies:
        copy.start()
    for copy in copies:
        copy.wait()


def fused(rhs_local, diag_inv, codes, row_scales, sep_index, live_rows, rhs_sep, root_inv):
    rhs_count, local_len = rhs_local.shape
    per_dev, block_len = diag_inv.shape[0], diag_inv.shape[1]
    coupled_rows = codes.shape[0]
    share, sep_len = root_inv.shape
    groups, tiles = lax.axis_size("grid"), lax.axis_size("tile")
    count = groups * tiles
    per_share = coupled_rows // tiles
    rpg = rhs_count // groups
    subs, pairs = rpg // ROWS, tiles // 2
    packed = pl.cdiv(subs * per_share, LANES) * LANES
    vmem = pl.BlockSpec(memory_space=pltpu.VMEM)
    scalar = pl.BlockSpec(memory_space=pltpu.SMEM)
    anywhere = pl.BlockSpec(memory_space=pl.ANY)
    dma = pltpu.SemaphoreType.DMA
    macs = rhs_count * local_len * 2 * (block_len + tiles * LANES)
    local, sep = pl.pallas_call(
        functools.partial(kernel, groups, tiles),
        out_shape=(
            jax.ShapeDtypeStruct((rhs_count, local_len), BF16),
            jax.ShapeDtypeStruct((subs, groups * ROWS, share), F32),
        ),
        in_specs=[scalar, vmem, vmem, vmem, anywhere, anywhere, anywhere, anywhere],
        out_specs=(anywhere, anywhere),
        scratch_shapes=[
            pltpu.VMEM((rhs_count, local_len), BF16),
            pltpu.VMEM(diag_inv.shape, BF16),
            pltpu.VMEM((tiles * LANES, local_len), BF16),
            pltpu.VMEM(root_inv.shape, BF16),
            pltpu.VMEM((rhs_count, local_len), BF16),
            pltpu.VMEM((tiles, groups * ROWS, packed), BF16),
            pltpu.VMEM((count, 1, LANES), jnp.int32),
            pltpu.VMEM((share, count * LANES), BF16),
            pltpu.VMEM((count, ROWS, packed), BF16),
            pltpu.VMEM((pairs, rpg, 2 * share), BF16),
            pltpu.VMEM((pairs, tiles, rpg, 2 * share), BF16),
            pltpu.VMEM((pairs, rpg, 2 * share), BF16),
            pltpu.VMEM((rpg, share), F32),
            pltpu.VMEM((subs, ROWS, share), F32),
            pltpu.VMEM((count, ROWS, packed), BF16),
            pltpu.VMEM((tiles, groups * ROWS, packed), BF16),
            pltpu.VMEM((rhs_count, local_len), F32),
            pltpu.VMEM((1, tiles * LANES), F32),
            pltpu.VMEM((tiles, 1, LANES), jnp.int32),
            pltpu.VMEM((rhs_count, local_len), BF16),
            pltpu.VMEM((subs, groups * ROWS, share), F32),
            dma((1 + per_dev,)),
            dma((2 + per_dev,)),
            dma((tiles,)),
            dma((4,)),
            dma((count,)),
            dma((count,)),
            dma((count,)),
            dma((count,)),
            dma((pairs,)),
            dma((pairs, tiles)),
            dma((pairs, tiles)),
            dma((pairs,)),
            dma((groups,)),
            dma((groups,)),
            dma((count,)),
            dma((count,)),
        ],
        compiler_params=pltpu.CompilerParams(
            collective_id=0, has_side_effects=True, vmem_limit_bytes=VMEM_BYTES
        ),
        cost_estimate=pl.CostEstimate(
            flops=2 * macs,
            bytes_accessed=2 * (diag_inv.size + codes.size + root_inv.size + 2 * rhs_local.size),
            transcendentals=0,
        ),
    )(
        live_rows,
        row_scales,
        sep_index,
        rhs_sep,
        rhs_local,
        diag_inv,
        codes,
        root_inv,
    )
    sep = sep.reshape(rhs_count, share)
    return pl.pallas_call(
        hand_over,
        out_shape=(
            jax.ShapeDtypeStruct(local.shape, BF16),
            jax.ShapeDtypeStruct(sep.shape, F32),
        ),
        in_specs=[anywhere, anywhere],
        out_specs=(anywhere, anywhere),
        scratch_shapes=[dma((2 * subs,))],
        compiler_params=pltpu.CompilerParams(vmem_limit_bytes=VMEM_BYTES),
    )(local, sep)


def fits(mesh, rhs_local, diag_inv, codes, root_inv):
    groups, tiles = mesh.shape["grid"], mesh.shape["tile"]
    rhs_count = rhs_local.shape[0]
    per_share = codes.shape[0] // (groups * tiles) // tiles
    share = root_inv.shape[0] // tiles
    return (
        rhs_count % (groups * ROWS) == 0
        and tiles % 2 == 0
        and per_share % ROWS == 0
        and per_share <= LANES
        and share % (LANES // 2) == 0
        and diag_inv.shape[1] % (2 * LANES) == 0 and codes.shape[0] // (groups * tiles) % LANES == 0
    )

def selector(offsets, share_len):
    columns = jnp.arange(share_len, dtype=jnp.int32)
    return (offsets[:, :, None] == columns[None, None, :]).astype(jnp.float32)


def on_device(rhs_local, diag_inv, codes, row_scales, sep_index, live_rows, rhs_sep, root_inv):
    rhs_count, local_len = rhs_local.shape
    per_dev, block_len = (diag_inv.shape[0], diag_inv.shape[1])
    coupled_rows = codes.shape[0]
    share_len, sep_len = root_inv.shape
    tile_count = lax.axis_size("tile")
    per_share = coupled_rows // tile_count
    pieces = []
    for block_pos in range(per_dev):
        columns = rhs_local[:, block_pos * block_len : (block_pos + 1) * block_len]
        pieces.append(jnp.dot(columns, diag_inv[block_pos], preferred_element_type=jnp.float32))
    forward_flat = jnp.concatenate(pieces, axis=1).astype(jnp.bfloat16)
    positions = jnp.arange(coupled_rows, dtype=jnp.int32)
    row_factor = row_scales * (positions < live_rows[0]).astype(jnp.float32)
    coupled = (
        lax.dot_general(
            forward_flat, codes, (((1,), (1,)), ((), ())), preferred_element_type=jnp.float32
        )
        * row_factor[None, :]
    )
    bases = (jnp.arange(tile_count, dtype=jnp.int32) * share_len)[:, None]
    local_offsets = sep_index.reshape(tile_count, per_share) - bases
    onehot = selector(local_offsets, share_len)
    values = coupled.reshape(rhs_count, tile_count, per_share)
    offsets = local_offsets.astype(jnp.float32)
    got_values, got_offsets = (
        lax.all_to_all(values, "tile", split_axis=1, concat_axis=1, tiled=True),
        lax.all_to_all(offsets[None], "tile", split_axis=1, concat_axis=1, tiled=True),
    )
    got_onehot = selector(got_offsets[0].astype(jnp.int32), share_len)
    own_share = jnp.einsum("rjp,jps->rs", got_values, got_onehot, precision=lax.Precision.HIGHEST)
    own_share = lax.psum(own_share, "grid")
    residue = (rhs_sep.astype(jnp.float32) - own_share).astype(jnp.bfloat16)
    root_part = jnp.dot(residue, root_inv, preferred_element_type=jnp.float32)
    forward_sep = lax.psum(root_part, "tile").astype(jnp.bfloat16)
    solved = lax.dot_general(
        forward_sep, root_inv, (((1,), (1,)), ((), ())), preferred_element_type=jnp.float32
    )
    gathered = lax.all_gather(solved.astype(jnp.bfloat16), "tile", axis=1, tiled=True)
    gathered_split = gathered.astype(jnp.float32).reshape(rhs_count, tile_count, share_len)
    picked = jnp.einsum(
        "rjs,jps->rjp", gathered_split, onehot, precision=lax.Precision.HIGHEST
    ).reshape(rhs_count, coupled_rows)
    weighted = (picked * row_factor[None, :]).astype(jnp.bfloat16)
    update = jnp.dot(weighted, codes, preferred_element_type=jnp.float32)
    misfit = (forward_flat.astype(jnp.float32) - update).astype(jnp.bfloat16)
    results = []
    for block_pos in range(per_dev):
        columns = misfit[:, block_pos * block_len : (block_pos + 1) * block_len]
        results.append(
            lax.dot_general(
                columns,
                diag_inv[block_pos],
                (((1,), (1,)), ((), ())),
                preferred_element_type=jnp.float32,
            )
        )
    result = jnp.concatenate(results, axis=1)
    return (result.astype(jnp.bfloat16), solved)


def solution(mesh):
    specs = (
        P(None, ("grid", "tile")),
        P(("grid", "tile"), None, None),
        P(("grid", "tile"), None),
        P(("grid", "tile")),
        P(("grid", "tile")),
        P(("grid", "tile")),
        P(None, "tile"),
        P("tile", None),
    )

    def run(*args):
        rhs_local, diag_inv, codes, root_inv = args[0], args[1], args[2], args[7]
        body = fused if fits(mesh, rhs_local, diag_inv, codes, root_inv) else on_device
        return jax.shard_map(
            body,
            mesh=mesh,
            in_specs=specs,
            out_specs=(P(None, ("grid", "tile")), P(None, "tile")),
            check_vma=False,
        )(*args)

    return run
```

```python
import functools

import jax
import jax.numpy as jnp
from jax import lax
from jax.experimental import pallas as pl
from jax.experimental.pallas import tpu as pltpu
from jax.sharding import PartitionSpec as P

LANES = 128
ROWS = 16
VMEM_BYTES = 54 * 1024 * 1024
MESH = pl.DeviceIdType.MESH
F32 = jnp.float32
BF16 = jnp.bfloat16
NT = (((1,), (1,)), ((), ()))


def lane_index(rows):
    return lax.broadcasted_iota(jnp.int32, (rows, LANES), 1)


def pack(pieces, length):
    tiles = [None] * pl.cdiv(len(pieces) * length, LANES)
    lane = lane_index(pieces[0].shape[0])

    def add(tile, piece):
        tiles[tile] = piece if tiles[tile] is None else tiles[tile] + piece

    for pos, piece in enumerate(pieces):
        tile, shift = pos * length // LANES, pos * length % LANES
        turned = pltpu.roll(piece, shift, 1) if shift else piece
        if shift + length > LANES:
            add(tile, jnp.where(lane >= shift, turned, 0.0))
            add(tile + 1, jnp.where(lane < shift, turned, 0.0))
        else:
            add(tile, turned)
    return jnp.concatenate(tiles, axis=1)


def unpack(packed, pieces, length):
    lane = lane_index(packed.shape[0])
    out = []
    for pos in range(pieces):
        tile, shift = pos * length // LANES, pos * length % LANES
        piece = packed[:, tile * LANES : (tile + 1) * LANES]
        if shift:
            piece = pltpu.roll(piece, LANES - shift, 1)
        if shift + length > LANES:
            rest = packed[:, (tile + 1) * LANES : (tile + 2) * LANES]
            piece = jnp.where(lane < LANES - shift, piece, pltpu.roll(rest, LANES - shift, 1))
        out.append(piece)
    return out


def kernel(
    groups,
    tiles,
    live_ref,
    scales_ref,
    places_ref,
    rhs_sep_ref,
    rhs_hbm,
    diag_hbm,
    codes_hbm,
    root_hbm,
    out_hbm,
    sep_hbm,
    rhs,
    diag,
    codes,
    root,
    forward,
    coupled,
    index_all,
    onehot,
    got,
    part,
    part_got,
    fsep,
    total,
    solved,
    picked,
    pick_got,
    update,
    factor_ref,
    index_ref,
    out_ref,
    sep_ref,
    store_sem,
    load_sem,
    code_sem,
    self_sem,
    idx_send,
    idx_recv,
    a_send,
    a_recv,
    r_send,
    r_recv,
    f_send,
    f_recv,
    s_send,
    s_recv,
    b_send,
    b_recv,
):
    g = lax.axis_index("grid")
    t = lax.axis_index("tile")
    count = groups * tiles
    mine = t * groups + g
    per_dev, block_len = diag.shape[0], diag.shape[1]
    share = root.shape[0]
    per_share = codes_hbm.shape[0] // tiles
    rhs_count = rhs.shape[0]
    rpg = rhs_count // groups
    subs = rpg // ROWS
    span = groups * ROWS
    pairs = tiles // 2
    wide = 2 * LANES
    fan = 2 * groups
    pair_me = t // 2
    toward = 1 - 2 * (2 * pair_me // pairs)

    def pair_at(distance):
        return lax.rem(pair_me + toward * distance + pairs, pairs)

    def lanes(position, size=LANES):
        return pl.ds(pl.multiple_of(position * size, size), size)

    def rows_of(group):
        return pl.ds(pl.multiple_of(group * ROWS, ROWS), ROWS)

    def halves(b):
        half = block_len // 2
        return [(b * block_len + h * half, b * block_len + (h + 1) * half) for h in range(2)]

    def device(slot):
        return (lax.rem(slot, groups), slot // groups)

    barrier = pltpu.get_barrier_semaphore()

    def greet(k, carry):
        pl.semaphore_signal(
            barrier, inc=1, device_id=device(lax.rem(mine + k, count)), device_id_type=MESH
        )
        return carry

    lax.fori_loop(1, count, greet, 0)

    loads = [pltpu.make_async_copy(rhs_hbm, rhs, load_sem.at[0])]
    for b in range(per_dev):
        loads.append(pltpu.make_async_copy(diag_hbm.at[b], diag.at[b], load_sem.at[1 + b]))
    for load in loads:
        load.start()
    code_loads = []
    for j in range(tiles):
        code_loads.append(
            pltpu.make_async_copy(
                codes_hbm.at[pl.ds(j * per_share, per_share)],
                codes.at[pl.ds(j * LANES, per_share)],
                code_sem.at[j],
            )
        )
    for load in code_loads:
        load.start()
    root_load = pltpu.make_async_copy(root_hbm, root, load_sem.at[1 + per_dev])
    root_load.start()
    if per_share < LANES:
        for j in range(tiles):
            codes[j * LANES + per_share : (j + 1) * LANES, :] = jnp.zeros(
                (LANES - per_share, codes.shape[1]), BF16
            )

    all_rows = scales_ref.shape[0]
    eight = (8, all_rows)
    scales = jnp.broadcast_to(scales_ref[...][None, :], eight)
    places = jnp.broadcast_to(places_ref[...][None, :], eight)
    position = lax.broadcasted_iota(jnp.int32, eight, 1)
    scales = jnp.where(position < live_ref[0], scales, 0.0)
    filled = lane_index(8) < per_share
    for j in range(tiles):
        shift = (all_rows - j * per_share) % all_rows
        turned = [pltpu.roll(x, shift, 1) if shift else x for x in (scales, places)]
        factor_ref[:, j * LANES : (j + 1) * LANES] = jnp.where(filled, turned[0][:, :LANES], 0.0)[:1]
        index_ref[j] = jnp.where(filled, turned[1][:, :LANES] - j * share, -1)[:1]

    loads[0].wait()
    for b in range(per_dev):
        loads[1 + b].wait()
        for low, high in halves(b):
            forward[:, low:high] = jnp.dot(
                rhs[:, b * block_len : high],
                diag[b, : high - b * block_len, low - b * block_len : high - b * block_len],
                preferred_element_type=F32,
            ).astype(BF16)

    pl.semaphore_wait(barrier, count - 1)

    def index_copy(peer, source):
        return pltpu.make_async_remote_copy(
            src_ref=index_ref.at[peer // groups],
            dst_ref=index_all.at[source],
            send_sem=idx_send.at[peer],
            recv_sem=idx_recv.at[source],
            device_id=device(peer),
            device_id_type=MESH,
        )

    def send_index(k, carry):
        index_copy(lax.rem(mine + k, count), mine).start()
        return carry

    lax.fori_loop(1, count, send_index, 0)
    own_index = pltpu.make_async_copy(index_ref.at[t], index_all.at[mine], self_sem.at[0])
    own_index.start()

    def term_copy(peer, source):
        return pltpu.make_async_remote_copy(
            src_ref=coupled.at[peer // groups, rows_of(lax.rem(peer, groups))],
            dst_ref=got.at[source],
            send_sem=a_send.at[peer],
            recv_sem=a_recv.at[source],
            device_id=device(peer),
            device_id_type=MESH,
        )

    for load in code_loads:
        load.wait()

    def couple(i, carry):
        q = pair_at(pairs - 1 - i)
        terms = lax.dot_general(
            forward[...], codes[lanes(q, wide), :], NT, preferred_element_type=F32
        )
        terms = terms * factor_ref[:, lanes(q, wide)]
        for u in range(2):
            ours = terms[:, u * LANES : (u + 1) * LANES]
            pieces = [ours[j * span : (j + 1) * span] for j in range(subs)]
            coupled[2 * q + u] = pack(pieces, per_share).astype(BF16)

        def send(k, inner):
            peer = q * fan + k

            @pl.when(peer != mine)
            def _():
                term_copy(peer, mine).start()

            return inner

        return lax.fori_loop(0, fan, send, carry)

    lax.fori_loop(0, pairs, couple, 0)
    own_terms = pltpu.make_async_copy(coupled.at[t, rows_of(g)], got.at[mine], self_sem.at[1])
    own_terms.start()

    own_index.wait()

    def index_done(k, carry):
        source = lax.rem(mine + k, count)
        index_copy(source, source).wait_recv()
        return carry

    lax.fori_loop(1, count, index_done, 0)

    def select(source, carry):
        places = lax.broadcasted_iota(jnp.int32, (share, LANES), 0)
        onehot[:, lanes(source)] = jnp.where(places == index_all[source], 1.0, 0.0).astype(BF16)
        return carry

    lax.fori_loop(0, count, select, 0)

    own_terms.wait()
    total[...] = jnp.zeros_like(total)

    def gather_terms(i, carry):
        q = pair_at(i)

        def arrived(k, inner):
            source = q * fan + k

            @pl.when(source != mine)
            def _():
                term_copy(source, source).wait_recv()

            return inner

        lax.fori_loop(0, fan, arrived, 0)
        columns = []
        for k in range(fan):
            pieces = unpack(got[q * fan + k].astype(F32), subs, per_share)
            columns.append(jnp.concatenate(pieces, axis=0).astype(BF16))
        total[...] += lax.dot_general(
            jnp.concatenate(columns, axis=1),
            onehot[:, lanes(q, fan * LANES)],
            NT,
            preferred_element_type=F32,
        )
        return carry

    lax.fori_loop(0, pairs, gather_terms, 0)
    rhs_sep = jnp.concatenate(
        [
            rhs_sep_ref[pl.ds(pl.multiple_of(j * span + g * ROWS, ROWS), ROWS), :]
            for j in range(subs)
        ],
        axis=0,
    )
    residue = (rhs_sep.astype(F32) - total[...]).astype(BF16)

    def owner_of(pair):
        return max(pair - 1, 0) * 2 + lax.rem(g, 2)

    def part_copy(pair, source):
        return pltpu.make_async_remote_copy(
            src_ref=part.at[pair],
            dst_ref=part_got.at[pair, source],
            send_sem=r_send.at[pair],
            recv_sem=r_recv.at[pair, source],
            device_id=(g, owner_of(pair)),
            device_id_type=MESH,
        )

    def block(pair):
        return slice(pair * 2 * share, (pair + 1) * 2 * share)

    root_load.wait()
    for pair in range(pairs - 1, -1, -1):

        @pl.when(t < 2 * pair + 2)
        def _():
            part[pair] = jnp.dot(
                residue, root[:, block(pair)], preferred_element_type=F32
            ).astype(BF16)

            @pl.when(t != owner_of(pair))
            def _():
                part_copy(pair, t).start()

    def fsep_copy(pair, peer):
        return pltpu.make_async_remote_copy(
            src_ref=fsep.at[pair],
            dst_ref=fsep.at[pair],
            send_sem=f_send.at[pair, peer],
            recv_sem=f_recv.at[pair],
            device_id=(g, peer),
            device_id_type=MESH,
        )

    for pair in range(pairs):

        @pl.when(t == owner_of(pair))
        def _():
            def add_part(k, summed):
                source = lax.rem(t + k, 2 * pair + 2)
                part_copy(pair, source).wait_recv()
                return summed + part_got[pair, source].astype(F32)

            summed = lax.fori_loop(1, 2 * pair + 2, add_part, part[pair].astype(F32))
            fsep[pair] = summed.astype(BF16)

            def send_fsep(k, carry):
                fsep_copy(pair, lax.rem(t + k, 2 * pair + 2)).start()
                return carry

            lax.fori_loop(1, 2 * pair + 2, send_fsep, 0)

    total[...] = jnp.zeros_like(total)
    for pair in range(pairs):

        @pl.when(t < 2 * pair + 2)
        def _():
            @pl.when(t != owner_of(pair))
            def _():
                fsep_copy(pair, t).wait_recv()

            total[...] += lax.dot_general(
                fsep[pair], root[:, block(pair)], NT, preferred_element_type=F32
            )

    for j in range(subs):
        solved[j] = total[j * ROWS : (j + 1) * ROWS, :]
    rounded = total[...].astype(BF16)

    def pick_copy(peer, source):
        return pltpu.make_async_remote_copy(
            src_ref=picked.at[peer],
            dst_ref=pick_got.at[source // groups, rows_of(lax.rem(source, groups))],
            send_sem=b_send.at[peer],
            recv_sem=b_recv.at[source],
            device_id=device(peer),
            device_id_type=MESH,
        )

    def pick(i, carry):
        q = pair_at(pairs - 1 - i)
        found = jnp.dot(rounded, onehot[:, lanes(q, fan * LANES)], preferred_element_type=F32)
        for k in range(fan):
            ours = found[:, k * LANES : (k + 1) * LANES]
            pieces = [ours[j * ROWS : (j + 1) * ROWS] for j in range(subs)]
            picked[q * fan + k] = pack(pieces, per_share).astype(BF16)

        def send(k, inner):
            peer = q * fan + k

            @pl.when(peer != mine)
            def _():
                pick_copy(peer, mine).start()

            return inner

        return lax.fori_loop(0, fan, send, carry)

    lax.fori_loop(0, pairs, pick, 0)
    own_pick = pltpu.make_async_copy(picked.at[mine], pick_got.at[t, rows_of(g)], self_sem.at[2])
    own_pick.start()

    def sep_copy(pg, source):
        return pltpu.make_async_remote_copy(
            src_ref=solved,
            dst_ref=sep_ref.at[:, rows_of(source)],
            send_sem=s_send.at[pg],
            recv_sem=s_recv.at[source],
            device_id=(pg, t),
            device_id_type=MESH,
        )

    def send_sep(k, carry):
        sep_copy(lax.rem(g + k, groups), g).start()
        return carry

    lax.fori_loop(1, groups, send_sep, 0)
    own_sep = pltpu.make_async_copy(solved, sep_ref.at[:, rows_of(g)], self_sem.at[3])
    own_sep.start()

    def early_sent(k, carry):
        peer = lax.rem(mine + k, count)
        index_copy(peer, mine).wait_send()
        term_copy(peer, mine).wait_send()
        return carry

    lax.fori_loop(1, count, early_sent, 0)
    for pair in range(pairs):

        @pl.when(jnp.logical_and(t < 2 * pair + 2, t != owner_of(pair)))
        def _():
            part_copy(pair, t).wait_send()

        @pl.when(t == owner_of(pair))
        def _():
            def fsep_sent(k, carry):
                fsep_copy(pair, lax.rem(t + k, 2 * pair + 2)).wait_send()
                return carry

            lax.fori_loop(1, 2 * pair + 2, fsep_sent, 0)

    own_pick.wait()
    update[...] = jnp.zeros_like(update)

    def gather_picks(i, carry):
        q = pair_at(i)

        def arrived(k, inner):
            source = q * fan + k

            @pl.when(source != mine)
            def _():
                pick_copy(source, source).wait_recv()

            return inner

        lax.fori_loop(0, fan, arrived, 0)
        columns = []
        for u in range(2):
            pieces = unpack(pick_got[2 * q + u].astype(F32), subs, per_share)
            columns.append(jnp.concatenate(pieces, axis=0))
        weighted = jnp.concatenate(columns, axis=1) * factor_ref[:, lanes(q, wide)]
        update[...] += jnp.dot(
            weighted.astype(BF16), codes[lanes(q, wide), :], preferred_element_type=F32
        )
        return carry

    lax.fori_loop(0, pairs, gather_picks, 0)
    own_sep.wait()

    def sep_done(k, carry):
        source = lax.rem(g + k, groups)
        sep_copy(source, source).wait_recv()
        sep_copy(source, g).wait_send()
        return carry

    lax.fori_loop(1, groups, sep_done, 0)

    stores = [pltpu.make_async_copy(sep_ref, sep_hbm, store_sem.at[per_dev])]
    stores[0].start()
    for b in range(per_dev):
        cols = slice(b * block_len, (b + 1) * block_len)
        misfit = (forward[:, cols].astype(F32) - update[:, cols]).astype(BF16)
        for low, high in halves(b):
            first = low - b * block_len
            out_ref[:, low:high] = lax.dot_general(
                misfit[:, first:],
                diag[b, first : high - b * block_len, first:],
                NT,
                preferred_element_type=F32,
            ).astype(BF16)
        stores.append(
            pltpu.make_async_copy(out_ref.at[:, cols], out_hbm.at[:, cols], store_sem.at[b])
        )
        stores[-1].start()

    def sent(k, carry):
        pick_copy(lax.rem(mine + k, count), mine).wait_send()
        return carry

    lax.fori_loop(1, count, sent, 0)
    for store in stores:
        store.wait()


def hand_over(local_in, sep_in, local_out, sep_out, local_held, sep_held, in_sems, out_sems):
    parts = in_sems.shape[0] // 2
    takes, gives = [], []
    for source, held, dest in (
        (local_in, local_held, local_out),
        (sep_in, sep_held, sep_out),
    ):
        rows = source.shape[0] // parts
        for part in range(parts):
            these, pos = pl.ds(part * rows, rows), len(takes)
            takes.append(
                pltpu.make_async_copy(source.at[these], held.at[these], in_sems.at[pos])
            )
            gives.append(pltpu.make_async_copy(held.at[these], dest.at[these], out_sems.at[pos]))
    for take in takes:
        take.start()
    for take, give in zip(takes, gives):
        take.wait()
        give.start()
    for give in gives:
        give.wait()


def fused(rhs_local, diag_inv, codes, row_scales, sep_index, live_rows, rhs_sep, root_inv):
    rhs_count, local_len = rhs_local.shape
    per_dev, block_len = diag_inv.shape[0], diag_inv.shape[1]
    coupled_rows = codes.shape[0]
    share, sep_len = root_inv.shape
    groups, tiles = lax.axis_size("grid"), lax.axis_size("tile")
    count = groups * tiles
    per_share = coupled_rows // tiles
    rpg = rhs_count // groups
    subs, pairs = rpg // ROWS, tiles // 2
    packed = pl.cdiv(subs * per_share, LANES) * LANES
    vmem = pl.BlockSpec(memory_space=pltpu.VMEM)
    scalar = pl.BlockSpec(memory_space=pltpu.SMEM)
    anywhere = pl.BlockSpec(memory_space=pl.ANY)
    dma = pltpu.SemaphoreType.DMA
    macs = rhs_count * local_len * 2 * (block_len + tiles * LANES)
    local, sep = pl.pallas_call(
        functools.partial(kernel, groups, tiles),
        out_shape=(
            jax.ShapeDtypeStruct((rhs_count, local_len), BF16),
            jax.ShapeDtypeStruct((subs, groups * ROWS, share), F32),
        ),
        in_specs=[scalar, vmem, vmem, vmem, anywhere, anywhere, anywhere, anywhere],
        out_specs=(anywhere, anywhere),
        scratch_shapes=[
            pltpu.VMEM((rhs_count, local_len), BF16),
            pltpu.VMEM(diag_inv.shape, BF16),
            pltpu.VMEM((tiles * LANES, local_len), BF16),
            pltpu.VMEM(root_inv.shape, BF16),
            pltpu.VMEM((rhs_count, local_len), BF16),
            pltpu.VMEM((tiles, groups * ROWS, packed), BF16),
            pltpu.VMEM((count, 1, LANES), jnp.int32),
            pltpu.VMEM((share, count * LANES), BF16),
            pltpu.VMEM((count, ROWS, packed), BF16),
            pltpu.VMEM((pairs, rpg, 2 * share), BF16),
            pltpu.VMEM((pairs, tiles, rpg, 2 * share), BF16),
            pltpu.VMEM((pairs, rpg, 2 * share), BF16),
            pltpu.VMEM((rpg, share), F32),
            pltpu.VMEM((subs, ROWS, share), F32),
            pltpu.VMEM((count, ROWS, packed), BF16),
            pltpu.VMEM((tiles, groups * ROWS, packed), BF16),
            pltpu.VMEM((rhs_count, local_len), F32),
            pltpu.VMEM((1, tiles * LANES), F32),
            pltpu.VMEM((tiles, 1, LANES), jnp.int32),
            pltpu.VMEM((rhs_count, local_len), BF16),
            pltpu.VMEM((subs, groups * ROWS, share), F32),
            dma((1 + per_dev,)),
            dma((2 + per_dev,)),
            dma((tiles,)),
            dma((4,)),
            dma((count,)),
            dma((count,)),
            dma((count,)),
            dma((count,)),
            dma((pairs,)),
            dma((pairs, tiles)),
            dma((pairs, tiles)),
            dma((pairs,)),
            dma((groups,)),
            dma((groups,)),
            dma((count,)),
            dma((count,)),
        ],
        compiler_params=pltpu.CompilerParams(
            collective_id=0, has_side_effects=True, vmem_limit_bytes=VMEM_BYTES
        ),
        cost_estimate=pl.CostEstimate(
            flops=2 * macs,
            bytes_accessed=2 * (diag_inv.size + codes.size + root_inv.size + 2 * rhs_local.size),
            transcendentals=0,
        ),
    )(
        live_rows,
        row_scales,
        sep_index,
        rhs_sep,
        rhs_local,
        diag_inv,
        codes,
        root_inv,
    )
    sep = sep.reshape(rhs_count, share)
    return pl.pallas_call(
        hand_over,
        out_shape=(
            jax.ShapeDtypeStruct(local.shape, BF16),
            jax.ShapeDtypeStruct(sep.shape, F32),
        ),
        in_specs=[anywhere, anywhere],
        out_specs=(anywhere, anywhere),
        scratch_shapes=[
            pltpu.VMEM(local.shape, BF16),
            pltpu.VMEM(sep.shape, F32),
            dma((2 * subs,)),
            dma((2 * subs,)),
        ],
        compiler_params=pltpu.CompilerParams(vmem_limit_bytes=VMEM_BYTES),
    )(local, sep)


def fits(mesh, rhs_local, diag_inv, codes, root_inv):
    groups, tiles = mesh.shape["grid"], mesh.shape["tile"]
    rhs_count = rhs_local.shape[0]
    per_share = codes.shape[0] // (groups * tiles) // tiles
    share = root_inv.shape[0] // tiles
    return (
        rhs_count % (groups * ROWS) == 0
        and tiles % 2 == 0
        and per_share % ROWS == 0
        and per_share <= LANES
        and share % (LANES // 2) == 0
        and diag_inv.shape[1] % (2 * LANES) == 0 and codes.shape[0] // (groups * tiles) % LANES == 0
    )

def selector(offsets, share_len):
    columns = jnp.arange(share_len, dtype=jnp.int32)
    return (offsets[:, :, None] == columns[None, None, :]).astype(jnp.float32)


def on_device(rhs_local, diag_inv, codes, row_scales, sep_index, live_rows, rhs_sep, root_inv):
    rhs_count, local_len = rhs_local.shape
    per_dev, block_len = (diag_inv.shape[0], diag_inv.shape[1])
    coupled_rows = codes.shape[0]
    share_len, sep_len = root_inv.shape
    tile_count = lax.axis_size("tile")
    per_share = coupled_rows // tile_count
    pieces = []
    for block_pos in range(per_dev):
        columns = rhs_local[:, block_pos * block_len : (block_pos + 1) * block_len]
        pieces.append(jnp.dot(columns, diag_inv[block_pos], preferred_element_type=jnp.float32))
    forward_flat = jnp.concatenate(pieces, axis=1).astype(jnp.bfloat16)
    positions = jnp.arange(coupled_rows, dtype=jnp.int32)
    row_factor = row_scales * (positions < live_rows[0]).astype(jnp.float32)
    coupled = (
        lax.dot_general(
            forward_flat, codes, (((1,), (1,)), ((), ())), preferred_element_type=jnp.float32
        )
        * row_factor[None, :]
    )
    bases = (jnp.arange(tile_count, dtype=jnp.int32) * share_len)[:, None]
    local_offsets = sep_index.reshape(tile_count, per_share) - bases
    onehot = selector(local_offsets, share_len)
    values = coupled.reshape(rhs_count, tile_count, per_share)
    offsets = local_offsets.astype(jnp.float32)
    got_values, got_offsets = (
        lax.all_to_all(values, "tile", split_axis=1, concat_axis=1, tiled=True),
        lax.all_to_all(offsets[None], "tile", split_axis=1, concat_axis=1, tiled=True),
    )
    got_onehot = selector(got_offsets[0].astype(jnp.int32), share_len)
    own_share = jnp.einsum("rjp,jps->rs", got_values, got_onehot, precision=lax.Precision.HIGHEST)
    own_share = lax.psum(own_share, "grid")
    residue = (rhs_sep.astype(jnp.float32) - own_share).astype(jnp.bfloat16)
    root_part = jnp.dot(residue, root_inv, preferred_element_type=jnp.float32)
    forward_sep = lax.psum(root_part, "tile").astype(jnp.bfloat16)
    solved = lax.dot_general(
        forward_sep, root_inv, (((1,), (1,)), ((), ())), preferred_element_type=jnp.float32
    )
    gathered = lax.all_gather(solved.astype(jnp.bfloat16), "tile", axis=1, tiled=True)
    gathered_split = gathered.astype(jnp.float32).reshape(rhs_count, tile_count, share_len)
    picked = jnp.einsum(
        "rjs,jps->rjp", gathered_split, onehot, precision=lax.Precision.HIGHEST
    ).reshape(rhs_count, coupled_rows)
    weighted = (picked * row_factor[None, :]).astype(jnp.bfloat16)
    update = jnp.dot(weighted, codes, preferred_element_type=jnp.float32)
    misfit = (forward_flat.astype(jnp.float32) - update).astype(jnp.bfloat16)
    results = []
    for block_pos in range(per_dev):
        columns = misfit[:, block_pos * block_len : (block_pos + 1) * block_len]
        results.append(
            lax.dot_general(
                columns,
                diag_inv[block_pos],
                (((1,), (1,)), ((), ())),
                preferred_element_type=jnp.float32,
            )
        )
    result = jnp.concatenate(results, axis=1)
    return (result.astype(jnp.bfloat16), solved)


def solution(mesh):
    specs = (
        P(None, ("grid", "tile")),
        P(("grid", "tile"), None, None),
        P(("grid", "tile"), None),
        P(("grid", "tile")),
        P(("grid", "tile")),
        P(("grid", "tile")),
        P(None, "tile"),
        P("tile", None),
    )

    def run(*args):
        rhs_local, diag_inv, codes, root_inv = args[0], args[1], args[2], args[7]
        body = fused if fits(mesh, rhs_local, diag_inv, codes, root_inv) else on_device
        return jax.shard_map(
            body,
            mesh=mesh,
            in_specs=specs,
            out_specs=(P(None, ("grid", "tile")), P(None, "tile")),
            check_vma=False,
        )(*args)

    return run
```
